128 devices in a mesh: row: 16 (over y, x), col: 8 (over z, core).
Axes of the slice: x: 4, y: 4, z: 4, core: 2. Of those that a mesh axis runs over, the one named last changes fastest.
Arguments:
- layer_input: bfloat16 [768, 8192], P('col', 'row'), may hold values from -6 to 6
- out_grad: bfloat16 [768, 8192], P('col', 'row'), may hold values from -4 to 4
- head_depth: int32 [768], P('col'), may hold values from 0 to 4
- gate_weight: bfloat16 [8192, 28672], P('row', 'col'), may hold values from -0.0625 to 0.0625
- up_weight: bfloat16 [8192, 28672], P('row', 'col'), may hold values from -0.0625 to 0.0625
- down_weight: bfloat16 [28672, 8192], P('col', 'row'), may hold values from -0.03125 to 0.03125
Outputs:
- grad_input: bfloat16 [768, 8192], P('col', 'row')
- grad_gate: bfloat16 [8192, 28672], P('row', 'col')
- grad_up: bfloat16 [8192, 28672], P('row', 'col')
- grad_down: bfloat16 [28672, 8192], P('col', 'row')
The draws below stay inside these ranges and needn't reach their ends.
All inputs are finite; a program needn't handle non-finite values.
Results may differ from the reference program's by a relative error of at most 0.033.
Values may be sent and summed in bfloat16 or wider, within the bound.
A program may use at most 128 MiB of HBM per device.

```python
import jax
import jax.numpy as jnp
from jax import lax

D = 8192
FF = 28672
TOKENS = 768
N_ROW = 16


def touch_ends(result, rng, low, high):
    longest = result.shape.index(max(result.shape))
    spots = []
    for shift in (0, 1):
        where = [jax.random.randint(jax.random.fold_in(rng, axis), (), 0, length) for axis, length in enumerate(result.shape)]
        where[longest] = (where[longest] + shift) % result.shape[longest]
        spots.append(tuple(where))
    return result.at[spots[0]].set(low).at[spots[1]].set(high)


def steps_of(key, shape, pieces, low, high):
    level = 1.0
    for position, shards_of in pieces:
        steps = jax.random.uniform(jax.random.fold_in(jax.random.fold_in(key, 6), position), (shards_of,), jnp.float32, low / len(pieces), high / len(pieces))
        level = level * jnp.repeat(jnp.exp(steps), shape[position] // shards_of).reshape((-1,) + (1,) * (len(shape) - 1 - position))
    return level


def centred(own_key, extent, width, limit, pieces=(), dtype=jnp.bfloat16):
    values = jax.random.normal(own_key, extent, jnp.float32) * width
    if len(pieces) > 0:
        values = steps_of(own_key, extent, pieces, -0.22, 0.18) * values
    return jnp.clip(values, min=-limit, max=limit).astype(dtype)


def setup_inputs(seed: int = 0) -> dict:
    arg_keys = jax.random.split(jax.random.key(seed), 7)
    layer_input = centred(arg_keys[0], (TOKENS, D), 1.0, 6.0, ((0, 8), (1, 16)))
    out_grad = centred(arg_keys[1], (TOKENS, D), 0.3, 4.0, ((0, 8), (1, 16)))
    head_depth = touch_ends(jax.random.randint(arg_keys[2], (TOKENS,), 0, 5), jax.random.fold_in(arg_keys[2], 1), 0, 4).astype(jnp.int32)
    gate_weight = centred(arg_keys[3], (D, FF), D ** -0.5, 0.0625, ((0, 16), (1, 8)))
    up_weight = centred(arg_keys[4], (D, FF), D ** -0.5, 0.0625, ((0, 16), (1, 8)))
    down_weight = centred(arg_keys[5], (FF, D), FF ** -0.5, 0.03125, ((0, 8), (1, 16)))
    return {"layer_input": layer_input, "out_grad": out_grad, "head_depth": head_depth, "gate_weight": gate_weight, "up_weight": up_weight, "down_weight": down_weight}


def rounded(value):
    return lax.optimization_barrier(value.astype(jnp.bfloat16)).astype(jnp.float32)


def reference(layer_input, out_grad, head_depth, gate_weight, up_weight, down_weight):
    weighting = jnp.power(jnp.float32(0.8), head_depth.astype(jnp.float32))
    scaled = (out_grad.astype(jnp.float32) * weighting[:, None]).astype(jnp.bfloat16)
    span_width = D // N_ROW
    gate_sum = jnp.zeros((TOKENS, FF), jnp.float32)
    up_sum = jnp.zeros((TOKENS, FF), jnp.float32)
    back_sum = jnp.zeros((TOKENS, FF), jnp.float32)
    for stripe in range(N_ROW):
        lower = stripe * span_width
        inputs_part = layer_input[:, lower:lower + span_width]
        grads_part = scaled[:, lower:lower + span_width]
        gate_sum = gate_sum + rounded(jnp.dot(inputs_part, gate_weight[lower:lower + span_width], preferred_element_type=jnp.float32))
        up_sum = up_sum + rounded(jnp.dot(inputs_part, up_weight[lower:lower + span_width], preferred_element_type=jnp.float32))
        back_sum = back_sum + rounded(lax.dot_general(grads_part, down_weight[:, lower:lower + span_width], (((1,), (1,)), ((), ())), preferred_element_type=jnp.float32))
    sigmoid_val = jax.nn.sigmoid(gate_sum)
    silu_val = gate_sum * sigmoid_val
    hidden = (silu_val * up_sum).astype(jnp.bfloat16)
    slope = sigmoid_val * (1.0 + gate_sum * (1.0 - sigmoid_val))
    gate_act = (back_sum * up_sum * slope).astype(jnp.bfloat16)
    up_act = (back_sum * silu_val).astype(jnp.bfloat16)
    contract_rows = (((0,), (0,)), ((), ()))
    contract_cols = (((1,), (1,)), ((), ()))
    grad_down = lax.dot_general(hidden, scaled, contract_rows, preferred_element_type=jnp.float32).astype(jnp.bfloat16)
    grad_gate = lax.dot_general(layer_input, gate_act, contract_rows, preferred_element_type=jnp.float32).astype(jnp.bfloat16)
    grad_up = lax.dot_general(layer_input, up_act, contract_rows, preferred_element_type=jnp.float32).astype(jnp.bfloat16)
    input_total = lax.dot_general(gate_act, gate_weight, contract_cols, preferred_element_type=jnp.float32)
    input_total = input_total + lax.dot_general(up_act, up_weight, contract_cols, preferred_element_type=jnp.float32)
    grad_input = input_total.astype(jnp.bfloat16)
    return grad_input, grad_gate, grad_up, grad_down
```

```python
import functools

import jax
import jax.numpy as jnp
from jax import lax
from jax.experimental import pallas as pl
from jax.experimental.pallas import tpu as pltpu
from jax.sharding import PartitionSpec as P

MESH = pl.DeviceIdType.MESH
BF = jnp.bfloat16
F32 = jnp.float32

T = 768
DB = 512
FB = 3584
TB = 96
PART = FB // 4
GROUPS = ((0, 384), (384, 256), (640, 256))
NG = len(GROUPS)
ROFF = (0, 384, 576, 672)

ORDER = (
    ("fwd", 0), ("fwd", 1),
    ("rs", 0, 0), ("fwd", 2), ("rs", 1, 0), ("rs", 0, 1), ("rs", 2, 0), ("rs", 1, 1), ("rs", 0, 2),
    ("rs", 0, 3), ("rs", 2, 1), ("rs", 1, 2), ("ag", 0, 3), ("rs", 1, 3), ("rs", 2, 2),
    ("ag", 0, 2), ("rs", 2, 3), ("ag", 1, 3), ("ag", 0, 1), ("ag", 2, 3), ("ag", 1, 2), ("ag", 2, 2),
    ("ag", 1, 1), ("ag", 0, 0), ("grad", 0), ("ag", 2, 1), ("ag", 1, 0), ("grad", 1), ("ag", 2, 0), ("grad", 2),
)


def nt(a, b):
    return lax.dot_general(a, b, (((1,), (1,)), ((), ())), preferred_element_type=F32)


def nn(a, b):
    return jnp.dot(a, b, preferred_element_type=F32)


def kernel(
    x_ref, og_ref, hd_ref, wg_hbm, wu_hbm, wd_hbm,
    gi_ref, dg_hbm, du_hbm, dd_hbm,
    S, R, XS, XT, WG, WU, WD, GI, GB, GR,
    wsem, zs, zr, cs, cr, ss, sr, gs, gr, osem, free,
):
    row = lax.axis_index("row")
    col = lax.axis_index("col")
    x = lax.rem(row, 4)
    y = row // 4
    z = col // 2
    c = lax.rem(col, 2)
    rows_of = (
        y * 4 + x + 1 - 2 * lax.rem(x, 2),
        (y + 1 - 2 * lax.rem(y, 2)) * 4 + x,
        y * 4 + 3 - x,
        (3 - y) * 4 + x,
    )
    bits = (lax.rem((x + 1) // 2, 2), lax.rem((y + 1) // 2, 2), x // 2, y // 2)

    def pick(values, d):
        return jnp.where(d == 0, values[0], jnp.where(d == 1, values[1], jnp.where(d == 2, values[2], values[3])))

    def low(p, k):
        at = jnp.int32(0)
        for i in range(k):
            at = at + pick(bits, lax.rem(p + i, 4)) * (T >> (i + 1))
        return at

    def columns(j, p):
        return pl.ds(pl.multiple_of(p * PART + GROUPS[j][0], 128), GROUPS[j][1])

    def rows(at, n):
        return pl.ds(pl.multiple_of(at, 48), n)

    def rs_copy(j, k, p):
        n = T >> (k + 1)
        at = low(p, k) + (1 - pick(bits, lax.rem(p + k, 4))) * n
        return pltpu.make_async_remote_copy(
            src_ref=S.at[:, rows(at, n), columns(j, p)],
            dst_ref=R.at[:, pl.ds(ROFF[k], n), columns(j, p)],
            send_sem=ss.at[j, k, p], recv_sem=sr.at[j, k, p],
            device_id=(pick(rows_of, lax.rem(p + k, 4)), col), device_id_type=MESH,
        )

    def ag_copy(j, k, p):
        n = T >> (k + 1)
        where = S.at[:, rows(low(p, k + 1), n), columns(j, p)]
        return pltpu.make_async_remote_copy(
            src_ref=where, dst_ref=where,
            send_sem=ss.at[j, 7 - k, p], recv_sem=sr.at[j, 7 - k, p],
            device_id=(pick(rows_of, lax.rem(p + k, 4)), col), device_id_type=MESH,
        )

    loads = [
        pltpu.make_async_copy(src, dst, wsem.at[i])
        for i, (src, dst) in enumerate(((wg_hbm, WG), (wu_hbm, WU), (wd_hbm, WD)))
    ]
    for load in loads:
        load.start()

    barrier = pltpu.get_barrier_semaphore()
    for r in rows_of:
        pl.semaphore_signal(barrier, inc=1, device_id=(r, col), device_id_type=MESH)
    others = []
    for dz in range(4):
        for dc in range(2):
            if dz + dc > 0:
                others.append((row, lax.rem(z + dz, 4) * 2 + lax.rem(c + dc, 2)))
    for device in others:
        pl.semaphore_signal(barrier, inc=1, device_id=device, device_id_type=MESH)

    depth = jnp.broadcast_to(hd_ref[...], (128, TB))
    weight = jnp.ones((128, TB), F32)
    for level in range(1, 5):
        weight = jnp.where(depth == level, F32(0.8) ** level, weight)
    weight = weight.T
    mine = pl.ds(pl.multiple_of(col * TB, TB), TB)
    XS[0, mine, :] = x_ref[...]
    for i in range(DB // 128):
        at = slice(i * 128, (i + 1) * 128)
        XS[1, mine, at] = (og_ref[:, at].astype(F32) * weight).astype(BF)

    pl.semaphore_wait(barrier, 11)

    def z_copy(dz):
        return pltpu.make_async_remote_copy(
            src_ref=XS.at[:, mine], dst_ref=XS.at[:, mine],
            send_sem=zs.at[dz], recv_sem=zr.at[dz],
            device_id=(row, lax.rem(z + dz, 4) * 2 + c), device_id_type=MESH,
        )

    def c_copy(dz):
        where = XS.at[:, pl.ds(pl.multiple_of((lax.rem(z + 4 - dz, 4) * 2 + c) * TB, TB), TB)]
        return pltpu.make_async_remote_copy(
            src_ref=where, dst_ref=where, send_sem=cs.at[dz], recv_sem=cr.at[dz],
            device_id=(row, z * 2 + 1 - c), device_id_type=MESH,
        )

    for dz in (1, 3, 2):
        z_copy(dz).start()
    c_copy(0).start()
    for dz in (1, 3, 2):
        z_copy(dz).wait_recv()
        c_copy(dz).start()
    for load in loads:
        load.wait()
    for dz in range(4):
        c_copy(dz).wait_recv()

    GI[...] = jnp.zeros_like(GI)

    def forward(j, p, at):
        r = rows(at, T // 2)
        cols = columns(j, p)
        S[0, r, cols] = nn(XS[0, r, :], WG[:, cols]).astype(BF)
        S[1, r, cols] = nn(XS[0, r, :], WU[:, cols]).astype(BF)
        S[2, r, cols] = nt(XS[1, r, :], WD[cols, :]).astype(BF)

    def fwd(j):
        @pl.loop(0, 4)
        def _(p):
            forward(j, p, (1 - pick(bits, p)) * (T // 2))
            rs_copy(j, 0, p).start()

        @pl.loop(0, 4)
        def _(p):
            forward(j, p, pick(bits, p) * (T // 2))

    def rs(j, k):
        n = T >> (k + 1)

        @pl.loop(0, 4)
        def _(p):
            rs_copy(j, k, p).wait_recv()
            cols = columns(j, p)
            at = low(p, k + 1)
            if k < 3:
                @pl.loop(0, n // 48)
                def _(i):
                    r = rows(at + i * 48, 48)
                    q = rows(ROFF[k] + i * 48, 48)
                    S[:, r, cols] = (S[:, r, cols].astype(F32) + R[:, q, cols].astype(F32)).astype(BF)

                rs_copy(j, k + 1, p).start()
            else:
                r = rows(at, 48)
                q = pl.ds(ROFF[3], 48)
                gate = S[0, r, cols].astype(F32) + R[0, q, cols].astype(F32)
                up = S[1, r, cols].astype(F32) + R[1, q, cols].astype(F32)
                back = S[2, r, cols].astype(F32) + R[2, q, cols].astype(F32)
                sig = jax.nn.sigmoid(gate)
                silu = gate * sig
                S[0, r, cols] = (silu * up).astype(BF)
                S[1, r, cols] = (back * up * (sig * (1.0 + gate * (1.0 - sig)))).astype(BF)
                S[2, r, cols] = (back * silu).astype(BF)
            rs_copy(j, k, p).wait_send()
            pl.semaphore_signal(
                free.at[j, k, p], inc=1,
                device_id=(pick(rows_of, lax.rem(p + k, 4)), col), device_id_type=MESH,
            )
        if k == 3:
            @pl.loop(0, 4)
            def _(p):
                gather(j, 3, p)

    def gather(j, k, p):
        pl.semaphore_wait(free.at[j, k, p], 1)
        ag_copy(j, k, p).start()

    def ag(j, k):
        @pl.loop(0, 4)
        def _(p):
            ag_copy(j, k, p).wait_recv()
            if k > 0:
                gather(j, k - 1, p)

    def out_copies(j, p):
        cols = columns(j, p)
        return (
            pltpu.make_async_copy(WG.at[:, cols], dg_hbm.at[:, cols], osem.at[j, 0, p]),
            pltpu.make_async_copy(WU.at[:, cols], du_hbm.at[:, cols], osem.at[j, 1, p]),
            pltpu.make_async_copy(WD.at[cols, :], dd_hbm.at[cols, :], osem.at[j, 2, p]),
        )

    def input_grad(j):
        @pl.loop(0, 4)
        def _(p):
            cols = columns(j, p)

            @pl.loop(0, 3)
            def _(i):
                r = pl.ds(pl.multiple_of(i * 256, 256), 256)
                GI[r, :] = GI[r, :] + nt(S[1, r, cols], WG[:, cols]) + nt(S[2, r, cols], WU[:, cols])

    def weight_grads(j):
        @pl.loop(0, 4)
        def _(p):
            cols = columns(j, p)
            WG[:, cols] = nn(XT[0], S[1, :, cols]).astype(BF)
            WU[:, cols] = nn(XT[0], S[2, :, cols]).astype(BF)
            WD[cols, :] = nn(XT[1], S[0, :, cols]).astype(BF).T
            for copy in out_copies(j, p):
                copy.start()

    def gi_copy(i):
        device = others[i]
        return pltpu.make_async_remote_copy(
            src_ref=GB.at[pl.ds(pl.multiple_of(device[1] * TB, TB), TB)], dst_ref=GR.at[i],
            send_sem=gs.at[i], recv_sem=gr.at[i], device_id=device, device_id_type=MESH,
        )

    for step in ORDER:
        what, j = step[:2]
        if what == "fwd":
            fwd(j)
            if j == NG - 1:
                XT[0] = XS[0].T
                XT[1] = XS[1].T
        elif what == "rs":
            rs(j, step[2])
        elif what == "ag":
            ag(j, step[2])
        else:
            input_grad(j)
            if j == NG - 1:
                GB[...] = GI[...].astype(BF)
                for i in range(7):
                    gi_copy(i).start()
            weight_grads(j)

    total = GI[mine, :]
    for i in range(7):
        gi_copy(i).wait_recv()
        total = total + GR[i].astype(F32)
    gi_ref[...] = total.astype(BF)

    for j in range(NG):
        @pl.loop(0, 4)
        def _(p):
            for copy in out_copies(j, p):
                copy.wait()
            for k in range(4):
                ag_copy(j, k, p).wait_send()
    for i in range(7):
        gi_copy(i).wait_send()
    for dz in range(4):
        if dz > 0:
            z_copy(dz).wait_send()
        c_copy(dz).wait_send()


def body(layer_input, out_grad, head_depth, gate_weight, up_weight, down_weight):
    vmem = pl.BlockSpec(memory_space=pltpu.VMEM)
    hbm = pl.BlockSpec(memory_space=pl.ANY)
    dma = pltpu.SemaphoreType.DMA
    return pl.pallas_call(
        kernel,
        out_shape=(
            jax.ShapeDtypeStruct((TB, DB), BF),
            jax.ShapeDtypeStruct((DB, FB), BF),
            jax.ShapeDtypeStruct((DB, FB), BF),
            jax.ShapeDtypeStruct((FB, DB), BF),
        ),
        in_specs=[vmem, vmem, vmem, hbm, hbm, hbm],
        out_specs=(vmem, hbm, hbm, hbm),
        scratch_shapes=[
            pltpu.VMEM((3, T, FB), BF),
            pltpu.VMEM((3, 720, FB), BF),
            pltpu.VMEM((2, T, DB), BF),
            pltpu.VMEM((2, DB, T), BF),
            pltpu.VMEM((DB, FB), BF),
            pltpu.VMEM((DB, FB), BF),
            pltpu.VMEM((FB, DB), BF),
            pltpu.VMEM((T, DB), F32),
            pltpu.VMEM((T, DB), BF),
            pltpu.VMEM((7, TB, DB), BF),
            dma((3,)), dma((4,)), dma((4,)), dma((4,)), dma((4,)),
            dma((NG, 8, 4)), dma((NG, 8, 4)), dma((7,)), dma((7,)), dma((NG, 3, 4)),
            pltpu.SemaphoreType.REGULAR((NG, 4, 4)),
        ],
        compiler_params=pltpu.CompilerParams(
            collective_id=0, has_side_effects=True, vmem_limit_bytes=62 * 2**20
        ),
        cost_estimate=pl.CostEstimate(
            flops=16 * T * DB * FB, bytes_accessed=12 * DB * FB, transcendentals=T * FB
        ),
    )(layer_input, out_grad, head_depth.reshape(1, TB), gate_weight, up_weight, down_weight)


def solution(mesh):
    in_specs = (
        P("col", "row"),
        P("col", "row"),
        P("col"),
        P("row", "col"),
        P("row", "col"),
        P("col", "row"),
    )
    out_specs = (P("col", "row"), P("row", "col"), P("row", "col"), P("col", "row"))
    return jax.shard_map(body, mesh=mesh, in_specs=in_specs, out_specs=out_specs, check_vma=False)
```

```python
import jax
import jax.numpy as jnp
from jax import lax
from jax.experimental import pallas as pl
from jax.experimental.pallas import tpu as pltpu
from jax.sharding import PartitionSpec as P

MESH = pl.DeviceIdType.MESH
BF = jnp.bfloat16
F32 = jnp.float32

T = 768
DB = 512
FB = 3584
TB = 96
PART = FB // 4
HALF = 384
W = 128
NP = 3
ROFF = ((0, 384, 576, 672), (0, 0, 384, 576))

ORDER = (
    ("relay", 0), ("relay", 1), ("all", 3), ("relay", 2), ("relay", 3), ("near", 0), ("relay", 4), ("near", 1),
    ("near", 2), ("near", 3), ("send", 1), ("rs", 3, 0), ("rs", 0, 1), ("send", 2), ("rs", 3, 1), ("rs", 0, 2),
    ("turn", 0), ("rs", 1, 1), ("rs", 3, 2), ("rs", 0, 3), ("rs", 1, 2), ("turn", 1), ("rs", 3, 3), ("rs", 2, 1),
    ("ag", 0, 3), ("rs", 1, 3), ("turn", 2), ("rs", 2, 2), ("ag", 0, 2), ("ag", 1, 3), ("turn", 3), ("rs", 2, 3),
    ("ag", 1, 2), ("turn", 4), ("ag", 2, 3),
    ("ag", 0, 1), ("in", 0), ("theirs", 0), ("ag", 2, 2), ("ag", 1, 1), ("in", 1), ("theirs", 1),
    ("ag", 3, 3), ("own", 0), ("ag", 3, 2),
    ("ag", 2, 1), ("in", 2), ("ag", 3, 1), ("theirs", 2), ("own", 1), ("fold", 1), ("fold", 2), ("fold", 3), ("fold", 4),
    ("ag", 3, 0), ("in", 3), ("own", 2), ("fold", 0), ("own", 3),
)


def nt(a, b):
    return lax.dot_general(a, b, (((1,), (1,)), ((), ())), preferred_element_type=F32)


def nn(a, b):
    return jnp.dot(a, b, preferred_element_type=F32)


def kernel(
    x_ref, og_ref, hd_ref, wg_hbm, wu_hbm, wd_hbm,
    gi_ref, dg_hbm, du_hbm, dd_hbm,
    S, R, XS, XT, WG, WU, WD, QG, QU, QD, GI, GB, CR, HS, ZR, YS, YR,
    wsem, xs, xr, qs, qr, zs, zr, cs, cr, ss, sr, gs, gr, osem, hs, hr, free,
):
    row = lax.axis_index("row")
    col = lax.axis_index("col")
    x = lax.rem(row, 4)
    y = row // 4
    z = col // 2
    c = lax.rem(col, 2)
    rows_of = (
        y * 4 + x + 1 - 2 * lax.rem(x, 2),
        (y + 1 - 2 * lax.rem(y, 2)) * 4 + x,
        y * 4 + 3 - x,
        (3 - y) * 4 + x,
    )
    bits = (lax.rem((x + 1) // 2, 2), lax.rem((y + 1) // 2, 2), x // 2, y // 2)

    def pick(values, d):
        return jnp.where(d == 0, values[0], jnp.where(d == 1, values[1], jnp.where(d == 2, values[2], values[3])))

    def near(d):
        return (pick(rows_of, lax.rem(d, 4)), col)

    def along_z(dz):
        return (row, lax.rem(z + dz, 4) * 2 + c)

    other_core = (row, z * 2 + 1 - c)

    def first(j):
        return 0 if j == NP else 1

    def size(j, k):
        return T >> (k + 1 - first(j))

    def low(j, p, k):
        at = jnp.int32(0)
        for i in range(first(j), k):
            at = at + pick(bits, lax.rem(p + i, 4)) * size(j, i)
        return at

    def rows(at, n):
        return pl.ds(pl.multiple_of(at, 48), n)

    def held(j, p):
        return pl.ds(pl.multiple_of(p * DB + j * W, W), W)

    def place(j, p):
        if j == NP:
            at = p * PART + 2 * HALF
        else:
            at = p * PART + pick(bits, p) * HALF + j * W
        return pl.ds(pl.multiple_of(at, W), W)

    def remote(src, dst, send, recv, device):
        return pltpu.make_async_remote_copy(
            src_ref=src, dst_ref=dst, send_sem=send, recv_sem=recv, device_id=device, device_id_type=MESH
        )

    def rs_copy(j, k, p):
        n = size(j, k)
        at = low(j, p, k) + (1 - pick(bits, lax.rem(p + k, 4))) * n
        return remote(
            S.at[j, p, :, rows(at, n)], R.at[j, p, :, pl.ds(ROFF[first(j)][k], n)],
            ss.at[j, k, p], sr.at[j, k, p], near(p + k),
        )

    def ag_copy(j, k, p):
        where = S.at[j, p, :, rows(low(j, p, k + 1), size(j, k))]
        return remote(where, where, ss.at[j, 7 - k, p], sr.at[j, 7 - k, p], near(p + k))

    def load_copies(p):
        copies = []
        for i, (at, n, to) in enumerate(
            ((p * PART + pick(bits, p) * HALF, HALF, p * DB), (p * PART + 2 * HALF, W, p * DB + HALF))
        ):
            src = pl.ds(pl.multiple_of(at, W), n)
            dst = pl.ds(pl.multiple_of(to, W), n)
            copies.append(pltpu.make_async_copy(wg_hbm.at[:, src], WG.at[:, dst], wsem.at[0, p, i]))
            copies.append(pltpu.make_async_copy(wu_hbm.at[:, src], WU.at[:, dst], wsem.at[1, p, i]))
            copies.append(pltpu.make_async_copy(wd_hbm.at[src], WD.at[dst], wsem.at[2, p, i]))
        return copies

    def weight_copies(p):
        at = pl.ds(pl.multiple_of(p * PART + (1 - pick(bits, p)) * HALF, W), HALF)
        return (
            remote(wg_hbm.at[:, at], QG.at[p], qs.at[0, p], qr.at[0, p], near(p)),
            remote(wu_hbm.at[:, at], QU.at[p], qs.at[1, p], qr.at[1, p], near(p)),
            remote(wd_hbm.at[at], QD.at[p], qs.at[2, p], qr.at[2, p], near(p)),
        )

    mine = pl.ds(pl.multiple_of(col * TB, TB), TB)

    def x_copy(d):
        return remote(XS.at[0, :, mine], XS.at[1 + d, :, mine], xs.at[d], xr.at[d], near(d))

    def block(dz):
        return pl.ds(pl.multiple_of((lax.rem(z + dz + 4, 4) * 2 + c) * TB, TB), TB)

    def z_copy(b, dz):
        where = XS.at[b, :, mine]
        return remote(where, where, zs.at[b, dz], zr.at[b, dz], along_z(dz))

    def z_relay(b, dz):
        where = XS.at[b, dz // 2, block(-dz)]
        return remote(where, where, zs.at[b, dz - 1], zr.at[b, dz - 1], along_z(dz))

    def c_copy(b, dz):
        where = XS.at[b, :, block(-dz)]
        return remote(where, where, cs.at[b, dz], cr.at[b, dz], other_core)

    barrier = pltpu.get_barrier_semaphore()
    for device in [near(d) for d in range(4)] + [along_z(dz) for dz in (1, 2, 3)] + [other_core]:
        pl.semaphore_signal(barrier, inc=1, device_id=device, device_id_type=MESH)

    @pl.loop(0, 4)
    def _(p):
        for copy in load_copies(p):
            copy.start()

    depth = jnp.broadcast_to(hd_ref[...], (128, TB))
    weight = jnp.ones((128, TB), F32)
    for level in range(1, 5):
        weight = jnp.where(depth == level, F32(0.8) ** level, weight)
    weight = weight.T
    XS[0, 0, mine, :] = x_ref[...]
    for i in range(DB // 128):
        at = slice(i * 128, (i + 1) * 128)
        XS[0, 1, mine, at] = (og_ref[:, at].astype(F32) * weight).astype(BF)

    pl.semaphore_wait(barrier, 8)

    for d in range(4):
        x_copy(d).start()
    for dz in (1, 3):
        z_copy(0, dz).start()
    c_copy(0, 0).start()
    for p in range(4):
        for copy in weight_copies(p):
            copy.start()
    GI[...] = jnp.zeros_like(GI)

    @pl.loop(0, 4)
    def _(d):
        x_copy(d).wait_recv()
        for dz in (1, 3):
            z_copy(1 + d, dz).start()
        c_copy(1 + d, 0).start()

    def relay(b):
        for dz in (1, 3):
            z_copy(b, dz).wait_recv()
            z_relay(b, dz).start()
            c_copy(b, dz).start()

    def gathered(b):
        for dz in (1, 3):
            z_relay(b, dz).wait_recv()
        c_copy(b, 2).start()
        for dz in range(4):
            c_copy(b, dz).wait_recv()

    def joined(parts):
        return jnp.concatenate(parts, axis=1)

    def forward_near(p, at):
        r = rows(at, T // 2)
        cols = pl.ds(p * DB, HALF)
        gate = nn(XS[0, 0, r, :], WG[:, cols]) + nn(XS[1 + p, 0, r, :], QG[p])
        up = nn(XS[0, 0, r, :], WU[:, cols]) + nn(XS[1 + p, 0, r, :], QU[p])
        back = nt(XS[0, 1, r, :], WD[cols, :]) + nt(XS[1 + p, 1, r, :], QD[p])
        for i, part in enumerate((gate, up, back)):
            for j in range(NP):
                S[j, p, i, r, :] = part[:, j * W : (j + 1) * W].astype(BF)

    def forward_all():
        gate_w = joined([WG[:, held(NP, p)] for p in range(4)])
        up_w = joined([WU[:, held(NP, p)] for p in range(4)])
        back_w = jnp.concatenate([WD[held(NP, p), :] for p in range(4)], axis=0)
        for i in range(2):
            r = slice(i * (T // 2), (i + 1) * (T // 2))
            parts = (nn(XS[0, 0, r, :], gate_w), nn(XS[0, 0, r, :], up_w), nt(XS[0, 1, r, :], back_w))
            for m, part in enumerate(parts):
                for p in range(4):
                    S[NP, p, m, r, :] = part[:, p * W : (p + 1) * W].astype(BF)

    def send(j):
        @pl.loop(0, 4)
        def _(p):
            rs_copy(j, first(j), p).start()

    def fwd_near(p):
        gathered(1 + p)
        for copy in weight_copies(p):
            copy.wait_recv()
        bit = pick(bits, lax.rem(p + 1, 4))
        forward_near(p, (1 - bit) * (T // 2))
        rs_copy(0, 1, p).start()
        forward_near(p, bit * (T // 2))

    def rs(j, k):
        n = size(j, k)
        step = min(n, 96)

        @pl.loop(0, 4)
        def _(p):
            rs_copy(j, k, p).wait_recv()
            at = low(j, p, k + 1)
            off = ROFF[first(j)][k]
            if k < 3:
                @pl.loop(0, n // step)
                def _(i):
                    r = rows(at + i * step, step)
                    q = rows(off + i * step, step)
                    S[j, p, :, r, :] = (S[j, p, :, r, :].astype(F32) + R[j, p, :, q, :].astype(F32)).astype(BF)

                rs_copy(j, k + 1, p).start()
            else:
                r = rows(at, n)
                q = pl.ds(off, n)
                gate = S[j, p, 0, r, :].astype(F32) + R[j, p, 0, q, :].astype(F32)
                up = S[j, p, 1, r, :].astype(F32) + R[j, p, 1, q, :].astype(F32)
                back = S[j, p, 2, r, :].astype(F32) + R[j, p, 2, q, :].astype(F32)
                sig = jax.nn.sigmoid(gate)
                silu = gate * sig
                S[j, p, 0, r, :] = (silu * up).astype(BF)
                S[j, p, 1, r, :] = (back * up * (sig * (1.0 + gate * (1.0 - sig)))).astype(BF)
                S[j, p, 2, r, :] = (back * silu).astype(BF)
            rs_copy(j, k, p).wait_send()
            pl.semaphore_signal(free.at[j, k, p], inc=1, device_id=near(p + k), device_id_type=MESH)

        if k == 3:
            @pl.loop(0, 4)
            def _(p):
                gather(j, 3, p)

    def gather(j, k, p):
        pl.semaphore_wait(free.at[j, k, p], 1)
        ag_copy(j, k, p).start()

    def ag(j, k):
        @pl.loop(0, 4)
        def _(p):
            ag_copy(j, k, p).wait_recv()
            if k > first(j):
                gather(j, k - 1, p)

    def own_copies(j, p):
        src, dst = held(j, p), place(j, p)
        return (
            pltpu.make_async_copy(WG.at[:, src], dg_hbm.at[:, dst], osem.at[0, j, p]),
            pltpu.make_async_copy(WU.at[:, src], du_hbm.at[:, dst], osem.at[1, j, p]),
            pltpu.make_async_copy(WD.at[src], dd_hbm.at[dst], osem.at[2, j, p]),
        )

    def near_copies(j, p):
        src, dst = pl.ds(j * W, W), place(j, p)
        return (
            remote(QG.at[p, :, src], dg_hbm.at[:, dst], gs.at[0, j, p], gr.at[0, j, p], near(p)),
            remote(QU.at[p, :, src], du_hbm.at[:, dst], gs.at[1, j, p], gr.at[1, j, p], near(p)),
            remote(QD.at[p, src], dd_hbm.at[dst], gs.at[2, j, p], gr.at[2, j, p], near(p)),
        )

    def input_grad(j):
        at = slice(j * W, (j + 1) * W)

        def acts(p, r):
            return [S[j, p, 1, r, :], S[j, p, 2, r, :]]

        weights = []
        for p in range(4):
            weights += [WG[:, held(j, p)], WU[:, held(j, p)]]
        weights = joined(weights)
        for i in range(3):
            r = slice(i * 256, (i + 1) * 256)
            GI[0, r, :] = GI[0, r, :] + nt(joined([a for p in range(4) for a in acts(p, r)]), weights)
        if j < NP:
            @pl.loop(0, 4)
            def _(p):
                both = joined([QG[p, :, at], QU[p, :, at]])
                for i in range(3):
                    r = slice(i * 256, (i + 1) * 256)
                    GI[1 + p, r, :] = GI[1 + p, r, :] + nt(joined(acts(p, r)), both)

    def near_grads(j):
        at = slice(j * W, (j + 1) * W)

        @pl.loop(0, 4)
        def _(p):
            both = nn(XT[1 + p, 0], joined([S[j, p, 1], S[j, p, 2]])).astype(BF)
            QG[p, :, at] = both[:, :W]
            QU[p, :, at] = both[:, W:]
            QD[p, at, :] = nn(XT[1 + p, 1], S[j, p, 0]).astype(BF).T
            for copy in near_copies(j, p):
                copy.start()

    def own_grads(j):
        @pl.loop(0, 2)
        def _(i):
            for p in (2 * i, 2 * i + 1):
                both = nn(XT[0, 0], joined([S[j, p, 1], S[j, p, 2]])).astype(BF)
                WG[:, held(j, p)] = both[:, :W]
                WU[:, held(j, p)] = both[:, W:]
            down = nn(XT[0, 1], joined([S[j, 2 * i, 0], S[j, 2 * i + 1, 0]])).astype(BF)
            for n, p in enumerate((2 * i, 2 * i + 1)):
                WD[held(j, p), :] = down[:, n * W : (n + 1) * W].T
                for copy in own_copies(j, p):
                    copy.start()

    def tokens(zz, cc):
        return pl.ds(pl.multiple_of((zz * 2 + cc) * TB, TB), TB)

    def gi_core(b):
        return remote(GB.at[b], CR.at[b], hs.at[0, b], hr.at[0, b], other_core)

    def gi_z(b, dz):
        return remote(HS.at[b, dz], ZR.at[b, dz], hs.at[dz, b], hr.at[dz, b], along_z(dz))

    def gi_near(d):
        return remote(YS.at[d], YR.at[d], hs.at[4, d], hr.at[4, d], near(d))

    def gi_send(b):
        for zz in range(4):
            GB[b, zz] = GI[b, tokens(zz, 1 - c), :].astype(BF)
        gi_core(b).start()

    def gi_fold(b):
        gi_core(b).wait_recv()
        for dz in (1, 3, 2):
            zz = lax.rem(z + dz, 4)
            HS[b, dz] = (GI[b, tokens(zz, c), :] + CR[b, zz].astype(F32)).astype(BF)
            gi_z(b, dz).start()

    def gi_total(b):
        total = GI[b, mine, :] + CR[b, z].astype(F32)
        for dz in (1, 3, 2):
            gi_z(b, dz).wait_recv()
            total = total + ZR[b, dz].astype(F32)
        return total

    for what, j, *level in ORDER:
        if what == "relay":
            relay(j)
        elif what == "all":
            gathered(0)
            for p in range(4):
                for copy in load_copies(p):
                    copy.wait()
            forward_all()
            send(NP)
        elif what == "send":
            send(j)
        elif what == "near":
            fwd_near(j)
        elif what == "turn":
            XT[j, 0] = XS[j, 0].T
            XT[j, 1] = XS[j, 1].T
        elif what == "rs":
            rs(j, level[0])
        elif what == "ag":
            ag(j, level[0])
        elif what == "in":
            input_grad(j)
            if j == NP - 1:
                @pl.loop(1, 5)
                def _(b):
                    gi_send(b)
            if j == NP:
                gi_send(0)
        elif what == "fold":
            gi_fold(j)
        elif what == "theirs":
            near_grads(j)
        else:
            own_grads(j)

    @pl.loop(0, 4)
    def _(d):
        YS[d] = gi_total(1 + d).astype(BF)
        gi_near(d).start()

    total = gi_total(0)
    for d in range(4):
        gi_near(d).wait_recv()
        total = total + YR[d].astype(F32)
    gi_ref[...] = total.astype(BF)

    @pl.loop(0, 4)
    def _(p):
        x_copy(p).wait_send()
        gi_near(p).wait_send()
        for copy in weight_copies(p):
            copy.wait_send()
        for j in range(NP + 1):
            for copy in own_copies(j, p):
                copy.wait()
            for k in range(first(j), 4):
                ag_copy(j, k, p).wait_send()
            if j < NP:
                for copy in near_copies(j, p):
                    copy.wait()

    @pl.loop(0, 5)
    def _(b):
        gi_core(b).wait_send()
        for dz in range(4):
            c_copy(b, dz).wait_send()
            if dz > 0:
                gi_z(b, dz).wait_send()
        for dz in (1, 3):
            z_copy(b, dz).wait_send()
            z_relay(b, dz).wait_send()


def body(layer_input, out_grad, head_depth, gate_weight, up_weight, down_weight):
    vmem = pl.BlockSpec(memory_space=pltpu.VMEM)
    hbm = pl.BlockSpec(memory_space=pl.ANY)
    dma = pltpu.SemaphoreType.DMA
    return pl.pallas_call(
        kernel,
        out_shape=(
            jax.ShapeDtypeStruct((TB, DB), BF),
            jax.ShapeDtypeStruct((DB, FB), BF),
            jax.ShapeDtypeStruct((DB, FB), BF),
            jax.ShapeDtypeStruct((FB, DB), BF),
        ),
        in_specs=[vmem, vmem, vmem, hbm, hbm, hbm],
        out_specs=(vmem, hbm, hbm, hbm),
        scratch_shapes=[
            pltpu.VMEM((NP + 1, 4, 3, T, W), BF),
            pltpu.VMEM((NP + 1, 4, 3, 720, W), BF),
            pltpu.VMEM((5, 2, T, DB), BF),
            pltpu.VMEM((5, 2, DB, T), BF),
            pltpu.VMEM((DB, 4 * DB), BF),
            pltpu.VMEM((DB, 4 * DB), BF),
            pltpu.VMEM((4 * DB, DB), BF),
            pltpu.VMEM((4, DB, HALF), BF),
            pltpu.VMEM((4, DB, HALF), BF),
            pltpu.VMEM((4, HALF, DB), BF),
            pltpu.VMEM((5, T, DB), F32),
            pltpu.VMEM((5, 4, TB, DB), BF),
            pltpu.VMEM((5, 4, TB, DB), BF),
            pltpu.VMEM((5, 4, TB, DB), BF),
            pltpu.VMEM((5, 4, TB, DB), BF),
            pltpu.VMEM((4, TB, DB), BF),
            pltpu.VMEM((4, TB, DB), BF),
            dma((3, 4, 2)), dma((4,)), dma((4,)), dma((3, 4)), dma((3, 4)),
            dma((5, 4)), dma((5, 4)), dma((5, 4)), dma((5, 4)),
            dma((NP + 1, 8, 4)), dma((NP + 1, 8, 4)), dma((3, NP, 4)), dma((3, NP, 4)),
            dma((3, NP + 1, 4)), dma((5, 5)), dma((5, 5)),
            pltpu.SemaphoreType.REGULAR((NP + 1, 4, 4)),
        ],
        compiler_params=pltpu.CompilerParams(
            collective_id=0, has_side_effects=True, vmem_limit_bytes=63 * 2**20
        ),
        cost_estimate=pl.CostEstimate(
            flops=16 * T * DB * FB, bytes_accessed=12 * DB * FB, transcendentals=T * FB
        ),
    )(layer_input, out_grad, head_depth.reshape(1, TB), gate_weight, up_weight, down_weight)


def solution(mesh):
    in_specs = (
        P("col", "row"),
        P("col", "row"),
        P("col"),
        P("row", "col"),
        P("row", "col"),
        P("col", "row"),
    )
    out_specs = (P("col", "row"), P("row", "col"), P("row", "col"), P("col", "row"))
    return jax.shard_map(body, mesh=mesh, in_specs=in_specs, out_specs=out_specs, check_vma=False)
```

```python
import jax
import jax.numpy as jnp
from jax import lax
from jax.experimental import pallas as pl
from jax.experimental.pallas import tpu as pltpu
from jax.sharding import PartitionSpec as P

MESH = pl.DeviceIdType.MESH
BF = jnp.bfloat16
F32 = jnp.float32

T = 768
DB = 512
FB = 3584
TB = 96
PART = FB // 4
HALF = 384
W = 128
NP = 3
ROFF = ((0, 384, 576, 672), (0, 0, 384, 576))

ORDER = (
    ("relay", 0), ("relay", 1), ("all", 3), ("relay", 2), ("near", 0, 0), ("near", 0, 1), ("relay", 3),
    ("near", 1, 0), ("near", 1, 1), ("relay", 4), ("near", 2, 0), ("near", 2, 1),
    ("near", 0, 2), ("near", 1, 2), ("near", 2, 2), ("near", 3, 0), ("near", 3, 1), ("near", 3, 2), ("send", 1),
    ("keep", 0), ("keep", 1), ("keep", 2), ("keep", 3),
    ("rs", 3, 0), ("rs", 0, 1), ("send", 2), ("rs", 3, 1), ("rs", 0, 2),
    ("turn", 0), ("rs", 1, 1), ("rs", 3, 2), ("rs", 0, 3), ("rs", 1, 2), ("turn", 1), ("rs", 3, 3), ("rs", 2, 1),
    ("ag", 0, 3), ("rs", 1, 3), ("turn", 2), ("rs", 2, 2), ("ag", 0, 2), ("ag", 1, 3), ("turn", 3), ("rs", 2, 3),
    ("ag", 1, 2), ("ag", 3, 3), ("turn", 4), ("ag", 2, 3),
    ("ag", 0, 1), ("in", 0), ("theirs", 0), ("ag", 2, 2), ("ag", 3, 2), ("ag", 1, 1), ("in", 1), ("own", 0),
    ("ag", 2, 1), ("ag", 3, 1), ("in", 2), ("theirs", 1), ("fold", 1), ("fold", 2), ("fold", 3), ("fold", 4),
    ("theirs", 2), ("own", 1), ("ag", 3, 0), ("in", 3), ("own", 2), ("fold", 0), ("own", 3),
)


def nt(a, b):
    return lax.dot_general(a, b, (((1,), (1,)), ((), ())), preferred_element_type=F32)


def nn(a, b):
    return jnp.dot(a, b, preferred_element_type=F32)


def kernel(
    x_ref, og_ref, hd_ref, wg_hbm, wu_hbm, wd_hbm,
    gi_ref, dg_hbm, du_hbm, dd_hbm,
    S, R, XS, XT, WG, WU, WD, QG, QU, QD, GI, GB, CR, HS, ZR, YS, YR,
    wsem, xs, xr, qs, qr, zs, zr, cs, cr, ss, sr, gs, gr, osem, hs, hr, free,
):
    row = lax.axis_index("row")
    col = lax.axis_index("col")
    x = lax.rem(row, 4)
    y = row // 4
    z = col // 2
    c = lax.rem(col, 2)
    rows_of = (
        y * 4 + x + 1 - 2 * lax.rem(x, 2),
        (y + 1 - 2 * lax.rem(y, 2)) * 4 + x,
        y * 4 + 3 - x,
        (3 - y) * 4 + x,
    )
    bits = (lax.rem((x + 1) // 2, 2), lax.rem((y + 1) // 2, 2), x // 2, y // 2)

    def pick(values, d):
        return jnp.where(d == 0, values[0], jnp.where(d == 1, values[1], jnp.where(d == 2, values[2], values[3])))

    def near(d):
        return (pick(rows_of, lax.rem(d, 4)), col)

    def along_z(dz):
        return (row, lax.rem(z + dz, 4) * 2 + c)

    other_core = (row, z * 2 + 1 - c)

    def first(j):
        return 0 if j == NP else 1

    def size(j, k):
        return T >> (k + 1 - first(j))

    def low(j, p, k):
        at = jnp.int32(0)
        for i in range(first(j), k):
            at = at + pick(bits, lax.rem(p + i, 4)) * size(j, i)
        return at

    def rows(at, n):
        return pl.ds(pl.multiple_of(at, 48), n)

    def held(j, p):
        return pl.ds(pl.multiple_of(p * DB + j * W, W), W)

    def place(j, p):
        if j == NP:
            at = p * PART + 2 * HALF
        else:
            at = p * PART + pick(bits, p) * HALF + j * W
        return pl.ds(pl.multiple_of(at, W), W)

    def remote(src, dst, send, recv, device):
        return pltpu.make_async_remote_copy(
            src_ref=src, dst_ref=dst, send_sem=send, recv_sem=recv, device_id=device, device_id_type=MESH
        )

    def rs_copy(j, k, p):
        n = size(j, k)
        at = low(j, p, k) + (1 - pick(bits, lax.rem(p + k, 4))) * n
        return remote(
            S.at[j, p, :, rows(at, n)], R.at[j, p, :, pl.ds(ROFF[first(j)][k], n)],
            ss.at[j, k, p], sr.at[j, k, p], near(p + k),
        )

    def ag_copy(j, k, p):
        where = S.at[j, p, :, rows(low(j, p, k + 1), size(j, k))]
        return remote(where, where, ss.at[j, 7 - k, p], sr.at[j, 7 - k, p], near(p + k))

    def load_copies(p):
        copies = []
        for i, (at, n, to) in enumerate(
            ((p * PART + pick(bits, p) * HALF, HALF, p * DB), (p * PART + 2 * HALF, W, p * DB + HALF))
        ):
            src = pl.ds(pl.multiple_of(at, W), n)
            dst = pl.ds(pl.multiple_of(to, W), n)
            copies.append(pltpu.make_async_copy(wg_hbm.at[:, src], WG.at[:, dst], wsem.at[0, p, i]))
            copies.append(pltpu.make_async_copy(wu_hbm.at[:, src], WU.at[:, dst], wsem.at[1, p, i]))
            copies.append(pltpu.make_async_copy(wd_hbm.at[src], WD.at[dst], wsem.at[2, p, i]))
        return copies

    def weight_copies(p):
        at = pl.ds(pl.multiple_of(p * PART + (1 - pick(bits, p)) * HALF, W), HALF)
        return (
            remote(wg_hbm.at[:, at], QG.at[p], qs.at[0, p], qr.at[0, p], near(p)),
            remote(wu_hbm.at[:, at], QU.at[p], qs.at[1, p], qr.at[1, p], near(p)),
            remote(wd_hbm.at[at], QD.at[p], qs.at[2, p], qr.at[2, p], near(p)),
        )

    mine = pl.ds(pl.multiple_of(col * TB, TB), TB)

    def x_copy(d):
        return remote(XS.at[0, :, mine], XS.at[1 + d, :, mine], xs.at[d], xr.at[d], near(d))

    def block(dz):
        return pl.ds(pl.multiple_of((lax.rem(z + dz + 4, 4) * 2 + c) * TB, TB), TB)

    def z_copy(b, dz):
        where = XS.at[b, :, mine]
        return remote(where, where, zs.at[b, dz], zr.at[b, dz], along_z(dz))

    def z_relay(b, dz):
        where = XS.at[b, dz // 2, block(-dz)]
        return remote(where, where, zs.at[b, dz - 1], zr.at[b, dz - 1], along_z(dz))

    def c_copy(b, dz):
        where = XS.at[b, :, block(-dz)]
        return remote(where, where, cs.at[b, dz], cr.at[b, dz], other_core)

    barrier = pltpu.get_barrier_semaphore()
    for device in [near(d) for d in range(4)] + [along_z(dz) for dz in (1, 2, 3)] + [other_core]:
        pl.semaphore_signal(barrier, inc=1, device_id=device, device_id_type=MESH)

    @pl.loop(0, 4)
    def _(p):
        for copy in load_copies(p):
            copy.start()

    depth = jnp.broadcast_to(hd_ref[...], (128, TB))
    weight = jnp.ones((128, TB), F32)
    for level in range(1, 5):
        weight = jnp.where(depth == level, F32(0.8) ** level, weight)
    weight = weight.T
    XS[0, 0, mine, :] = x_ref[...]
    for i in range(DB // 128):
        at = slice(i * 128, (i + 1) * 128)
        XS[0, 1, mine, at] = (og_ref[:, at].astype(F32) * weight).astype(BF)

    pl.semaphore_wait(barrier, 8)

    for d in range(4):
        x_copy(d).start()
    for dz in (1, 3):
        z_copy(0, dz).start()
    c_copy(0, 0).start()
    for p in range(4):
        for copy in weight_copies(p):
            copy.start()
    GI[...] = jnp.zeros_like(GI)

    def z_send(b):
        for dz in (1, 3):
            z_copy(b, dz).start()

    def relay(b):
        for dz in (1, 3):
            z_copy(b, dz).wait_recv()
            z_relay(b, dz).start()
            c_copy(b, dz).start()
        if b == 0:
            for d in range(4):
                x_copy(d).wait_recv()
                c_copy(1 + d, 0).start()
                if d < 2:
                    z_send(1 + d)
        elif b < 3:
            z_send(b + 2)

    def gathered(b):
        for dz in (1, 3):
            z_relay(b, dz).wait_recv()
        c_copy(b, 2).start()
        for dz in range(4):
            c_copy(b, dz).wait_recv()

    def joined(parts):
        return jnp.concatenate(parts, axis=1)

    def forward_near(p, m, at):
        r = rows(at, T // 2)
        cols = pl.ds(p * DB, HALF)
        if m < 2:
            near_w, own_w = ((QG, WG), (QU, WU))[m]
            part = nn(XS[0, 0, r, :], own_w[:, cols]) + nn(XS[1 + p, 0, r, :], near_w[p])
        else:
            part = nt(XS[0, 1, r, :], WD[cols, :]) + nt(XS[1 + p, 1, r, :], QD[p])
        for j in range(NP):
            S[j, p, m, r, :] = part[:, j * W : (j + 1) * W].astype(BF)

    def forward_all():
        gate_w = joined([WG[:, held(NP, p)] for p in range(4)])
        up_w = joined([WU[:, held(NP, p)] for p in range(4)])
        back_w = jnp.concatenate([WD[held(NP, p), :] for p in range(4)], axis=0)
        for i in range(2):
            r = slice(i * (T // 2), (i + 1) * (T // 2))
            parts = (nn(XS[0, 0, r, :], gate_w), nn(XS[0, 0, r, :], up_w), nt(XS[0, 1, r, :], back_w))
            for m, part in enumerate(parts):
                for p in range(4):
                    S[NP, p, m, r, :] = part[:, p * W : (p + 1) * W].astype(BF)

    def send(j):
        @pl.loop(0, 4)
        def _(p):
            rs_copy(j, first(j), p).start()

    def fwd_near(p, m):
        if m == 0:
            gathered(1 + p)
        weight_copies(p)[m].wait_recv()
        bit = pick(bits, lax.rem(p + 1, 4))
        forward_near(p, m, (1 - bit) * (T // 2))
        if m == 2:
            rs_copy(0, 1, p).start()
        else:
            forward_near(p, m, bit * (T // 2))

    def fwd_kept(p):
        forward_near(p, 2, pick(bits, lax.rem(p + 1, 4)) * (T // 2))

    def rs(j, k):
        n = size(j, k)
        step = min(n, 96)

        @pl.loop(0, 4)
        def _(p):
            rs_copy(j, k, p).wait_recv()
            at = low(j, p, k + 1)
            off = ROFF[first(j)][k]
            if k < 3:
                @pl.loop(0, n // step)
                def _(i):
                    r = rows(at + i * step, step)
                    q = rows(off + i * step, step)
                    S[j, p, :, r, :] = (S[j, p, :, r, :].astype(F32) + R[j, p, :, q, :].astype(F32)).astype(BF)

                rs_copy(j, k + 1, p).start()
            else:
                r = rows(at, n)
                q = pl.ds(off, n)
                gate = S[j, p, 0, r, :].astype(F32) + R[j, p, 0, q, :].astype(F32)
                up = S[j, p, 1, r, :].astype(F32) + R[j, p, 1, q, :].astype(F32)
                back = S[j, p, 2, r, :].astype(F32) + R[j, p, 2, q, :].astype(F32)
                sig = jax.nn.sigmoid(gate)
                silu = gate * sig
                S[j, p, 0, r, :] = (silu * up).astype(BF)
                S[j, p, 1, r, :] = (back * up * (sig * (1.0 + gate * (1.0 - sig)))).astype(BF)
                S[j, p, 2, r, :] = (back * silu).astype(BF)
            rs_copy(j, k, p).wait_send()
            pl.semaphore_signal(free.at[j, k, p], inc=1, device_id=near(p + k), device_id_type=MESH)

        if k == 3:
            @pl.loop(0, 4)
            def _(p):
                gather(j, 3, p)

    def gather(j, k, p):
        pl.semaphore_wait(free.at[j, k, p], 1)
        ag_copy(j, k, p).start()

    def ag(j, k):
        @pl.loop(0, 4)
        def _(p):
            ag_copy(j, k, p).wait_recv()
            if k > first(j):
                gather(j, k - 1, p)

    def own_copies(j, p):
        src, dst = held(j, p), place(j, p)
        return (
            pltpu.make_async_copy(WG.at[:, src], dg_hbm.at[:, dst], osem.at[0, j, p]),
            pltpu.make_async_copy(WU.at[:, src], du_hbm.at[:, dst], osem.at[1, j, p]),
            pltpu.make_async_copy(WD.at[src], dd_hbm.at[dst], osem.at[2, j, p]),
        )

    def near_copies(j, p):
        src, dst = pl.ds(j * W, W), place(j, p)
        return (
            remote(QG.at[p, :, src], dg_hbm.at[:, dst], gs.at[0, j, p], gr.at[0, j, p], near(p)),
            remote(QU.at[p, :, src], du_hbm.at[:, dst], gs.at[1, j, p], gr.at[1, j, p], near(p)),
            remote(QD.at[p, src], dd_hbm.at[dst], gs.at[2, j, p], gr.at[2, j, p], near(p)),
        )

    def input_grad(j):
        at = slice(j * W, (j + 1) * W)

        def acts(p, r):
            return [S[j, p, 1, r, :], S[j, p, 2, r, :]]

        weights = []
        for p in range(4):
            weights += [WG[:, held(j, p)], WU[:, held(j, p)]]
        weights = joined(weights)
        for i in range(3):
            r = slice(i * 256, (i + 1) * 256)
            GI[0, r, :] = GI[0, r, :] + nt(joined([a for p in range(4) for a in acts(p, r)]), weights)
        if j < NP:
            @pl.loop(0, 4)
            def _(p):
                both = joined([QG[p, :, at], QU[p, :, at]])
                for i in range(3):
                    r = slice(i * 256, (i + 1) * 256)
                    GI[1 + p, r, :] = GI[1 + p, r, :] + nt(joined(acts(p, r)), both)

    def near_grads(j):
        at = slice(j * W, (j + 1) * W)

        @pl.loop(0, 4)
        def _(p):
            both = nn(XT[1 + p, 0], joined([S[j, p, 1], S[j, p, 2]])).astype(BF)
            QG[p, :, at] = both[:, :W]
            QU[p, :, at] = both[:, W:]
            QD[p, at, :] = nn(XT[1 + p, 1], S[j, p, 0]).astype(BF).T
            for copy in near_copies(j, p):
                copy.start()

    def own_grads(j):
        @pl.loop(0, 2)
        def _(i):
            for p in (2 * i, 2 * i + 1):
                both = nn(XT[0, 0], joined([S[j, p, 1], S[j, p, 2]])).astype(BF)
                WG[:, held(j, p)] = both[:, :W]
                WU[:, held(j, p)] = both[:, W:]
            down = nn(XT[0, 1], joined([S[j, 2 * i, 0], S[j, 2 * i + 1, 0]])).astype(BF)
            for n, p in enumerate((2 * i, 2 * i + 1)):
                WD[held(j, p), :] = down[:, n * W : (n + 1) * W].T
                for copy in own_copies(j, p):
                    copy.start()

    def tokens(zz, cc):
        return pl.ds(pl.multiple_of((zz * 2 + cc) * TB, TB), TB)

    def gi_core(b):
        return remote(GB.at[b], CR.at[b], hs.at[0, b], hr.at[0, b], other_core)

    def gi_z(b, dz):
        return remote(HS.at[b, dz], ZR.at[b, dz], hs.at[dz, b], hr.at[dz, b], along_z(dz))

    def gi_near(d):
        return remote(YS.at[d], YR.at[d], hs.at[4, d], hr.at[4, d], near(d))

    def gi_send(b):
        for zz in range(4):
            GB[b, zz] = GI[b, tokens(zz, 1 - c), :].astype(BF)
        gi_core(b).start()

    def gi_fold(b):
        gi_core(b).wait_recv()
        for dz in (1, 3, 2):
            zz = lax.rem(z + dz, 4)
            HS[b, dz] = (GI[b, tokens(zz, c), :] + CR[b, zz].astype(F32)).astype(BF)
            gi_z(b, dz).start()

    def gi_total(b):
        total = GI[b, mine, :] + CR[b, z].astype(F32)
        for dz in (1, 3, 2):
            gi_z(b, dz).wait_recv()
            total = total + ZR[b, dz].astype(F32)
        return total

    for what, j, *level in ORDER:
        if what == "relay":
            relay(j)
        elif what == "all":
            gathered(0)
            for p in range(4):
                for copy in load_copies(p):
                    copy.wait()
            forward_all()
            send(NP)
        elif what == "send":
            send(j)
        elif what == "near":
            fwd_near(j, level[0])
        elif what == "keep":
            fwd_kept(j)
        elif what == "turn":
            XT[j, 0] = XS[j, 0].T
            XT[j, 1] = XS[j, 1].T
        elif what == "rs":
            rs(j, level[0])
        elif what == "ag":
            ag(j, level[0])
        elif what == "in":
            input_grad(j)
            if j == NP - 1:
                @pl.loop(1, 5)
                def _(b):
                    gi_send(b)
            if j == NP:
                gi_send(0)
        elif what == "fold":
            gi_fold(j)
        elif what == "theirs":
            near_grads(j)
        else:
            own_grads(j)

    @pl.loop(0, 4)
    def _(d):
        YS[d] = gi_total(1 + d).astype(BF)
        gi_near(d).start()

    total = gi_total(0)
    for d in range(4):
        gi_near(d).wait_recv()
        total = total + YR[d].astype(F32)
    gi_ref[...] = total.astype(BF)

    @pl.loop(0, 4)
    def _(p):
        x_copy(p).wait_send()
        gi_near(p).wait_send()
        for copy in weight_copies(p):
            copy.wait_send()
        for j in range(NP + 1):
            for copy in own_copies(j, p):
                copy.wait()
            for k in range(first(j), 4):
                ag_copy(j, k, p).wait_send()
            if j < NP:
                for copy in near_copies(j, p):
                    copy.wait()

    @pl.loop(0, 5)
    def _(b):
        gi_core(b).wait_send()
        for dz in range(4):
            c_copy(b, dz).wait_send()
            if dz > 0:
                gi_z(b, dz).wait_send()
        for dz in (1, 3):
            z_copy(b, dz).wait_send()
            z_relay(b, dz).wait_send()


def copy_kernel(a, b, c, d, out_a, out_b, out_c, out_d, held_a, held_b, held_c, held_d, sem):
    pieces = [(a, held_a, out_a)]
    for src, mid, dst in ((b, held_b, out_b), (c, held_c, out_c), (d, held_d, out_d)):
        n = src.shape[0] // 4
        for k in range(4):
            at = pl.ds(k * n, n)
            pieces.append((src.at[at], mid.at[at], dst.at[at]))
    reads = [pltpu.make_async_copy(src, mid, sem.at[0, i]) for i, (src, mid, dst) in enumerate(pieces)]
    writes = [pltpu.make_async_copy(mid, dst, sem.at[1, i]) for i, (src, mid, dst) in enumerate(pieces)]
    for read in reads:
        read.start()
    for read, write in zip(reads, writes):
        read.wait()
        write.start()
    for write in writes:
        write.wait()


def body(layer_input, out_grad, head_depth, gate_weight, up_weight, down_weight):
    vmem = pl.BlockSpec(memory_space=pltpu.VMEM)
    hbm = pl.BlockSpec(memory_space=pl.ANY)
    dma = pltpu.SemaphoreType.DMA
    outs = pl.pallas_call(
        kernel,
        out_shape=(
            jax.ShapeDtypeStruct((TB, DB), BF),
            jax.ShapeDtypeStruct((DB, FB), BF),
            jax.ShapeDtypeStruct((DB, FB), BF),
            jax.ShapeDtypeStruct((FB, DB), BF),
        ),
        in_specs=[vmem, vmem, vmem, hbm, hbm, hbm],
        out_specs=(vmem, hbm, hbm, hbm),
        scratch_shapes=[
            pltpu.VMEM((NP + 1, 4, 3, T, W), BF),
            pltpu.VMEM((NP + 1, 4, 3, 720, W), BF),
            pltpu.VMEM((5, 2, T, DB), BF),
            pltpu.VMEM((5, 2, DB, T), BF),
            pltpu.VMEM((DB, 4 * DB), BF),
            pltpu.VMEM((DB, 4 * DB), BF),
            pltpu.VMEM((4 * DB, DB), BF),
            pltpu.VMEM((4, DB, HALF), BF),
            pltpu.VMEM((4, DB, HALF), BF),
            pltpu.VMEM((4, HALF, DB), BF),
            pltpu.VMEM((5, T, DB), F32),
            pltpu.VMEM((5, 4, TB, DB), BF),
            pltpu.VMEM((5, 4, TB, DB), BF),
            pltpu.VMEM((5, 4, TB, DB), BF),
            pltpu.VMEM((5, 4, TB, DB), BF),
            pltpu.VMEM((4, TB, DB), BF),
            pltpu.VMEM((4, TB, DB), BF),
            dma((3, 4, 2)), dma((4,)), dma((4,)), dma((3, 4)), dma((3, 4)),
            dma((5, 4)), dma((5, 4)), dma((5, 4)), dma((5, 4)),
            dma((NP + 1, 8, 4)), dma((NP + 1, 8, 4)), dma((3, NP, 4)), dma((3, NP, 4)),
            dma((3, NP + 1, 4)), dma((5, 5)), dma((5, 5)),
            pltpu.SemaphoreType.REGULAR((NP + 1, 4, 4)),
        ],
        compiler_params=pltpu.CompilerParams(
            collective_id=0, has_side_effects=True, vmem_limit_bytes=63 * 2**20
        ),
        cost_estimate=pl.CostEstimate(
            flops=16 * T * DB * FB, bytes_accessed=12 * DB * FB, transcendentals=T * FB
        ),
    )(layer_input, out_grad, head_depth.reshape(1, TB), gate_weight, up_weight, down_weight)
    return pl.pallas_call(
        copy_kernel,
        out_shape=[jax.ShapeDtypeStruct(out.shape, out.dtype) for out in outs],
        in_specs=[hbm] * 4,
        out_specs=[hbm] * 4,
        scratch_shapes=[pltpu.VMEM(out.shape, out.dtype) for out in outs] + [dma((2, 13))],
        compiler_params=pltpu.CompilerParams(vmem_limit_bytes=63 * 2**20),
        cost_estimate=pl.CostEstimate(flops=0, bytes_accessed=12 * DB * FB, transcendentals=0),
    )(*outs)


def solution(mesh):
    in_specs = (
        P("col", "row"),
        P("col", "row"),
        P("col"),
        P("row", "col"),
        P("row", "col"),
        P("col", "row"),
    )
    out_specs = (P("col", "row"), P("row", "col"), P("row", "col"), P("col", "row"))
    return jax.shard_map(body, mesh=mesh, in_specs=in_specs, out_specs=out_specs, check_vma=False)
```

```python
import jax
import jax.numpy as jnp
from jax import lax
from jax.experimental import pallas as pl
from jax.experimental.pallas import tpu as pltpu
from jax.sharding import PartitionSpec as P

MESH = pl.DeviceIdType.MESH
BF = jnp.bfloat16
F32 = jnp.float32

T = 768
DB = 512
FB = 3584
TB = 96
PART = FB // 4
HALF = 384
W = 128
NP = 3
ROFF = ((0, 384, 576, 672), (0, 0, 384, 576))

ORDER = (
    ("relay", 0), ("relay", 1), ("all", 3), ("relay", 2), ("near", 0, 0), ("near", 0, 1), ("relay", 3),
    ("near", 1, 0), ("near", 1, 1), ("relay", 4), ("near", 2, 0), ("near", 2, 1),
    ("near", 0, 2), ("near", 1, 2), ("near", 2, 2), ("near", 3, 0), ("near", 3, 1), ("near", 3, 2), ("send", 1),
    ("keep", 0), ("keep", 1), ("keep", 2), ("keep", 3),
    ("rs", 3, 0), ("rs", 0, 1), ("send", 2), ("rs", 3, 1), ("rs", 0, 2),
    ("turn", 0), ("rs", 1, 1), ("rs", 3, 2), ("rs", 0, 3), ("rs", 1, 2), ("turn", 1), ("rs", 3, 3), ("rs", 2, 1),
    ("ag", 0, 3), ("rs", 1, 3), ("turn", 2), ("rs", 2, 2), ("ag", 0, 2), ("ag", 1, 3), ("turn", 3), ("rs", 2, 3),
    ("ag", 1, 2), ("ag", 3, 3), ("turn", 4), ("ag", 2, 3),
    ("ag", 0, 1), ("in", 0), ("ag", 2, 2), ("theirs", 0), ("ag", 3, 2), ("ag", 1, 1), ("in", 1),
    ("ag", 2, 1), ("ag", 3, 1), ("in", 2), ("fold", 1), ("fold", 2), ("fold", 3), ("fold", 4), ("theirs", 1),
    ("theirs", 2), ("own", 0), ("ag", 3, 0), ("in", 3), ("own", 1), ("fold", 0), ("own", 2), ("own", 3),
)


def nt(a, b):
    return lax.dot_general(a, b, (((1,), (1,)), ((), ())), preferred_element_type=F32)


def nn(a, b):
    return jnp.dot(a, b, preferred_element_type=F32)


def kernel(
    x_ref, og_ref, hd_ref, wg_hbm, wu_hbm, wd_hbm,
    gi_ref, dg_hbm, du_hbm, dd_hbm,
    S, R, XS, XT, WG, WU, WD, QG, QU, QD, GI, GB, CR, HS, ZR, YS, YR,
    wsem, xs, xr, qs, qr, zs, zr, cs, cr, ss, sr, gs, gr, osem, hs, hr, free,
):
    row = lax.axis_index("row")
    col = lax.axis_index("col")
    x = lax.rem(row, 4)
    y = row // 4
    z = col // 2
    c = lax.rem(col, 2)
    rows_of = (
        y * 4 + x + 1 - 2 * lax.rem(x, 2),
        (y + 1 - 2 * lax.rem(y, 2)) * 4 + x,
        y * 4 + 3 - x,
        (3 - y) * 4 + x,
    )
    bits = (lax.rem((x + 1) // 2, 2), lax.rem((y + 1) // 2, 2), x // 2, y // 2)

    def pick(values, d):
        return jnp.where(d == 0, values[0], jnp.where(d == 1, values[1], jnp.where(d == 2, values[2], values[3])))

    def near(d):
        return (pick(rows_of, lax.rem(d, 4)), col)

    def along_z(dz):
        return (row, lax.rem(z + dz, 4) * 2 + c)

    other_core = (row, z * 2 + 1 - c)

    def first(j):
        return 0 if j == NP else 1

    def size(j, k):
        return T >> (k + 1 - first(j))

    def low(j, p, k):
        at = jnp.int32(0)
        for i in range(first(j), k):
            at = at + pick(bits, lax.rem(p + i, 4)) * size(j, i)
        return at

    def rows(at, n):
        return pl.ds(pl.multiple_of(at, 48), n)

    def held(j, p):
        return pl.ds(pl.multiple_of(p * DB + j * W, W), W)

    def place(j, p):
        if j == NP:
            at = p * PART + 2 * HALF
        else:
            at = p * PART + pick(bits, p) * HALF + j * W
        return pl.ds(pl.multiple_of(at, W), W)

    def remote(src, dst, send, recv, device):
        return pltpu.make_async_remote_copy(
            src_ref=src, dst_ref=dst, send_sem=send, recv_sem=recv, device_id=device, device_id_type=MESH
        )

    def rs_copy(j, k, p):
        n = size(j, k)
        at = low(j, p, k) + (1 - pick(bits, lax.rem(p + k, 4))) * n
        return remote(
            S.at[j, p, :, rows(at, n)], R.at[j, p, :, pl.ds(ROFF[first(j)][k], n)],
            ss.at[j, k, p], sr.at[j, k, p], near(p + k),
        )

    def ag_copy(j, k, p):
        where = S.at[j, p, :, rows(low(j, p, k + 1), size(j, k))]
        return remote(where, where, ss.at[j, 7 - k, p], sr.at[j, 7 - k, p], near(p + k))

    def load_copies(p):
        copies = []
        for i, (at, n, to) in enumerate(
            ((p * PART + pick(bits, p) * HALF, HALF, p * DB), (p * PART + 2 * HALF, W, p * DB + HALF))
        ):
            src = pl.ds(pl.multiple_of(at, W), n)
            dst = pl.ds(pl.multiple_of(to, W), n)
            copies.append(pltpu.make_async_copy(wg_hbm.at[:, src], WG.at[:, dst], wsem.at[0, p, i]))
            copies.append(pltpu.make_async_copy(wu_hbm.at[:, src], WU.at[:, dst], wsem.at[1, p, i]))
            copies.append(pltpu.make_async_copy(wd_hbm.at[src], WD.at[dst], wsem.at[2, p, i]))
        return copies

    def weight_copies(p):
        at = pl.ds(pl.multiple_of(p * PART + (1 - pick(bits, p)) * HALF, W), HALF)
        return (
            remote(wg_hbm.at[:, at], QG.at[p], qs.at[0, p], qr.at[0, p], near(p)),
            remote(wu_hbm.at[:, at], QU.at[p], qs.at[1, p], qr.at[1, p], near(p)),
            remote(wd_hbm.at[at], QD.at[p], qs.at[2, p], qr.at[2, p], near(p)),
        )

    mine = pl.ds(pl.multiple_of(col * TB, TB), TB)

    def x_copy(d):
        return remote(XS.at[0, :, mine], XS.at[1 + d, :, mine], xs.at[d], xr.at[d], near(d))

    def block(dz):
        return pl.ds(pl.multiple_of((lax.rem(z + dz + 4, 4) * 2 + c) * TB, TB), TB)

    def z_copy(b, dz):
        where = XS.at[b, :, mine]
        return remote(where, where, zs.at[b, dz], zr.at[b, dz], along_z(dz))

    def z_relay(b, dz):
        where = XS.at[b, dz // 2, block(-dz)]
        return remote(where, where, zs.at[b, dz - 1], zr.at[b, dz - 1], along_z(dz))

    def c_copy(b, dz):
        where = XS.at[b, :, block(-dz)]
        return remote(where, where, cs.at[b, dz], cr.at[b, dz], other_core)

    barrier = pltpu.get_barrier_semaphore()
    for device in [near(d) for d in range(4)] + [along_z(dz) for dz in (1, 2, 3)] + [other_core]:
        pl.semaphore_signal(barrier, inc=1, device_id=device, device_id_type=MESH)

    @pl.loop(0, 4)
    def _(p):
        for copy in load_copies(p):
            copy.start()

    depth = jnp.broadcast_to(hd_ref[...], (128, TB))
    weight = jnp.ones((128, TB), F32)
    for level in range(1, 5):
        weight = jnp.where(depth == level, F32(0.8) ** level, weight)
    weight = weight.T
    XS[0, 0, mine, :] = x_ref[...]
    for i in range(DB // 128):
        at = slice(i * 128, (i + 1) * 128)
        XS[0, 1, mine, at] = (og_ref[:, at].astype(F32) * weight).astype(BF)

    pl.semaphore_wait(barrier, 8)

    for d in range(4):
        x_copy(d).start()
    for dz in (1, 3):
        z_copy(0, dz).start()
    c_copy(0, 0).start()
    for p in range(4):
        for copy in weight_copies(p):
            copy.start()
    GI[...] = jnp.zeros_like(GI)

    def z_send(b):
        for dz in (1, 3):
            z_copy(b, dz).start()

    def relay(b):
        for dz in (1, 3):
            z_copy(b, dz).wait_recv()
            z_relay(b, dz).start()
            c_copy(b, dz).start()
        if b == 0:
            for d in range(4):
                x_copy(d).wait_recv()
                c_copy(1 + d, 0).start()
                if d < 2:
                    z_send(1 + d)
        elif b < 3:
            z_send(b + 2)

    def gathered(b):
        for dz in (1, 3):
            z_relay(b, dz).wait_recv()
        c_copy(b, 2).start()
        for dz in range(4):
            c_copy(b, dz).wait_recv()

    def joined(parts):
        return jnp.concatenate(parts, axis=1)

    def forward_near(p, m, at):
        r = rows(at, T // 2)
        cols = pl.ds(p * DB, HALF)
        if m < 2:
            near_w, own_w = ((QG, WG), (QU, WU))[m]
            part = nn(XS[0, 0, r, :], own_w[:, cols]) + nn(XS[1 + p, 0, r, :], near_w[p])
        else:
            part = nt(XS[0, 1, r, :], WD[cols, :]) + nt(XS[1 + p, 1, r, :], QD[p])
        for j in range(NP):
            S[j, p, m, r, :] = part[:, j * W : (j + 1) * W].astype(BF)

    def forward_all():
        gate_w = joined([WG[:, held(NP, p)] for p in range(4)])
        up_w = joined([WU[:, held(NP, p)] for p in range(4)])
        back_w = jnp.concatenate([WD[held(NP, p), :] for p in range(4)], axis=0)
        for i in range(2):
            r = slice(i * (T // 2), (i + 1) * (T // 2))
            parts = (nn(XS[0, 0, r, :], gate_w), nn(XS[0, 0, r, :], up_w), nt(XS[0, 1, r, :], back_w))
            for m, part in enumerate(parts):
                for p in range(4):
                    S[NP, p, m, r, :] = part[:, p * W : (p + 1) * W].astype(BF)

    def send(j):
        @pl.loop(0, 4)
        def _(p):
            rs_copy(j, first(j), p).start()

    def fwd_near(p, m):
        if m == 0:
            gathered(1 + p)
        weight_copies(p)[m].wait_recv()
        bit = pick(bits, lax.rem(p + 1, 4))
        forward_near(p, m, (1 - bit) * (T // 2))
        if m == 2:
            rs_copy(0, 1, p).start()
        else:
            forward_near(p, m, bit * (T // 2))

    def fwd_kept(p):
        forward_near(p, 2, pick(bits, lax.rem(p + 1, 4)) * (T // 2))

    def rs(j, k):
        n = size(j, k)
        step = min(n, 96)

        @pl.loop(0, 4)
        def _(p):
            rs_copy(j, k, p).wait_recv()
            at = low(j, p, k + 1)
            off = ROFF[first(j)][k]
            if k < 3:
                @pl.loop(0, n // step)
                def _(i):
                    r = rows(at + i * step, step)
                    q = rows(off + i * step, step)
                    S[j, p, :, r, :] = (S[j, p, :, r, :].astype(F32) + R[j, p, :, q, :].astype(F32)).astype(BF)

                rs_copy(j, k + 1, p).start()
            else:
                r = rows(at, n)
                q = pl.ds(off, n)
                gate = S[j, p, 0, r, :].astype(F32) + R[j, p, 0, q, :].astype(F32)
                up = S[j, p, 1, r, :].astype(F32) + R[j, p, 1, q, :].astype(F32)
                back = S[j, p, 2, r, :].astype(F32) + R[j, p, 2, q, :].astype(F32)
                sig = jax.nn.sigmoid(gate)
                silu = gate * sig
                S[j, p, 0, r, :] = (silu * up).astype(BF)
                S[j, p, 1, r, :] = (back * up * (sig * (1.0 + gate * (1.0 - sig)))).astype(BF)
                S[j, p, 2, r, :] = (back * silu).astype(BF)
            rs_copy(j, k, p).wait_send()
            pl.semaphore_signal(free.at[j, k, p], inc=1, device_id=near(p + k), device_id_type=MESH)

        if k == 3:
            @pl.loop(0, 4)
            def _(p):
                gather(j, 3, p)

    def gather(j, k, p):
        pl.semaphore_wait(free.at[j, k, p], 1)
        ag_copy(j, k, p).start()

    def ag(j, k):
        @pl.loop(0, 4)
        def _(p):
            ag_copy(j, k, p).wait_recv()
            if k > first(j):
                gather(j, k - 1, p)

    def own_copies(j, p):
        src, dst = held(j, p), place(j, p)
        return (
            pltpu.make_async_copy(WG.at[:, src], dg_hbm.at[:, dst], osem.at[0, j, p]),
            pltpu.make_async_copy(WU.at[:, src], du_hbm.at[:, dst], osem.at[1, j, p]),
            pltpu.make_async_copy(WD.at[src], dd_hbm.at[dst], osem.at[2, j, p]),
        )

    def near_copies(j, p):
        src, dst = pl.ds(j * W, W), place(j, p)
        return (
            remote(QG.at[p, :, src], dg_hbm.at[:, dst], gs.at[0, j, p], gr.at[0, j, p], near(p)),
            remote(QU.at[p, :, src], du_hbm.at[:, dst], gs.at[1, j, p], gr.at[1, j, p], near(p)),
            remote(QD.at[p, src], dd_hbm.at[dst], gs.at[2, j, p], gr.at[2, j, p], near(p)),
        )

    def input_grad(j):
        at = slice(j * W, (j + 1) * W)

        def acts(p, r):
            return [S[j, p, 1, r, :], S[j, p, 2, r, :]]

        if j < NP:
            @pl.loop(0, 4)
            def _(p):
                both = joined([QG[p, :, at], QU[p, :, at]])
                for i in range(3):
                    r = slice(i * 256, (i + 1) * 256)
                    GI[1 + p, r, :] = GI[1 + p, r, :] + nt(joined(acts(p, r)), both)
                if j == NP - 1:
                    gi_send(1 + p)

        weights = []
        for p in range(4):
            weights += [WG[:, held(j, p)], WU[:, held(j, p)]]
        weights = joined(weights)
        for i in range(3):
            r = slice(i * 256, (i + 1) * 256)
            GI[0, r, :] = GI[0, r, :] + nt(joined([a for p in range(4) for a in acts(p, r)]), weights)
        if j == NP:
            gi_send(0)

    def near_grads(j):
        at = slice(j * W, (j + 1) * W)

        @pl.loop(0, 4)
        def _(p):
            both = nn(XT[1 + p, 0], joined([S[j, p, 1], S[j, p, 2]])).astype(BF)
            QG[p, :, at] = both[:, :W]
            QU[p, :, at] = both[:, W:]
            QD[p, at, :] = nn(XT[1 + p, 1], S[j, p, 0]).astype(BF).T
            for copy in near_copies(j, p):
                copy.start()

    def own_grads(j):
        @pl.loop(0, 2)
        def _(i):
            for p in (2 * i, 2 * i + 1):
                both = nn(XT[0, 0], joined([S[j, p, 1], S[j, p, 2]])).astype(BF)
                WG[:, held(j, p)] = both[:, :W]
                WU[:, held(j, p)] = both[:, W:]
            down = nn(XT[0, 1], joined([S[j, 2 * i, 0], S[j, 2 * i + 1, 0]])).astype(BF)
            for n, p in enumerate((2 * i, 2 * i + 1)):
                WD[held(j, p), :] = down[:, n * W : (n + 1) * W].T
                for copy in own_copies(j, p):
                    copy.start()

    def tokens(zz, cc):
        return pl.ds(pl.multiple_of((zz * 2 + cc) * TB, TB), TB)

    def gi_core(b):
        return remote(GB.at[b], CR.at[b], hs.at[0, b], hr.at[0, b], other_core)

    def gi_z(b, dz):
        return remote(HS.at[b, dz], ZR.at[b, dz], hs.at[dz, b], hr.at[dz, b], along_z(dz))

    def gi_near(d):
        return remote(YS.at[d], YR.at[d], hs.at[4, d], hr.at[4, d], near(d))

    def gi_send(b):
        for zz in range(4):
            GB[b, zz] = GI[b, tokens(zz, 1 - c), :].astype(BF)
        gi_core(b).start()

    def gi_fold(b):
        gi_core(b).wait_recv()
        for dz in (1, 3, 2):
            zz = lax.rem(z + dz, 4)
            HS[b, dz] = (GI[b, tokens(zz, c), :] + CR[b, zz].astype(F32)).astype(BF)
            gi_z(b, dz).start()

    def gi_total(b):
        total = GI[b, mine, :] + CR[b, z].astype(F32)
        for dz in (1, 3, 2):
            gi_z(b, dz).wait_recv()
            total = total + ZR[b, dz].astype(F32)
        return total

    for what, j, *level in ORDER:
        if what == "relay":
            relay(j)
        elif what == "all":
            gathered(0)
            for p in range(4):
                for copy in load_copies(p):
                    copy.wait()
            forward_all()
            send(NP)
        elif what == "send":
            send(j)
        elif what == "near":
            fwd_near(j, level[0])
        elif what == "keep":
            fwd_kept(j)
        elif what == "turn":
            XT[j, 0] = XS[j, 0].T
            XT[j, 1] = XS[j, 1].T
        elif what == "rs":
            rs(j, level[0])
        elif what == "ag":
            ag(j, level[0])
        elif what == "in":
            input_grad(j)
        elif what == "fold":
            gi_fold(j)
        elif what == "theirs":
            near_grads(j)
        else:
            own_grads(j)

    @pl.loop(0, 4)
    def _(d):
        YS[d] = gi_total(1 + d).astype(BF)
        gi_near(d).start()

    total = gi_total(0)
    for d in range(4):
        gi_near(d).wait_recv()
        total = total + YR[d].astype(F32)
    gi_ref[...] = total.astype(BF)

    @pl.loop(0, 4)
    def _(p):
        x_copy(p).wait_send()
        gi_near(p).wait_send()
        for copy in weight_copies(p):
            copy.wait_send()
        for j in range(NP + 1):
            for copy in own_copies(j, p):
                copy.wait()
            for k in range(first(j), 4):
                ag_copy(j, k, p).wait_send()
            if j < NP:
                for copy in near_copies(j, p):
                    copy.wait()

    @pl.loop(0, 5)
    def _(b):
        gi_core(b).wait_send()
        for dz in range(4):
            c_copy(b, dz).wait_send()
            if dz > 0:
                gi_z(b, dz).wait_send()
        for dz in (1, 3):
            z_copy(b, dz).wait_send()
            z_relay(b, dz).wait_send()


def copy_kernel(a, b, c, d, out_a, out_b, out_c, out_d, held_a, held_b, held_c, held_d, sem):
    pieces = [(a, held_a, out_a)]
    for src, mid, dst in ((b, held_b, out_b), (c, held_c, out_c), (d, held_d, out_d)):
        n = src.shape[0] // 4
        for k in range(4):
            at = pl.ds(k * n, n)
            pieces.append((src.at[at], mid.at[at], dst.at[at]))
    reads = [pltpu.make_async_copy(src, mid, sem.at[0, i]) for i, (src, mid, dst) in enumerate(pieces)]
    writes = [pltpu.make_async_copy(mid, dst, sem.at[1, i]) for i, (src, mid, dst) in enumerate(pieces)]
    for read in reads:
        read.start()
    for read, write in zip(reads, writes):
        read.wait()
        write.start()
    for write in writes:
        write.wait()


def body(layer_input, out_grad, head_depth, gate_weight, up_weight, down_weight):
    vmem = pl.BlockSpec(memory_space=pltpu.VMEM)
    hbm = pl.BlockSpec(memory_space=pl.ANY)
    dma = pltpu.SemaphoreType.DMA
    outs = pl.pallas_call(
        kernel,
        out_shape=(
            jax.ShapeDtypeStruct((TB, DB), BF),
            jax.ShapeDtypeStruct((DB, FB), BF),
            jax.ShapeDtypeStruct((DB, FB), BF),
            jax.ShapeDtypeStruct((FB, DB), BF),
        ),
        in_specs=[vmem, vmem, vmem, hbm, hbm, hbm],
        out_specs=(vmem, hbm, hbm, hbm),
        scratch_shapes=[
            pltpu.VMEM((NP + 1, 4, 3, T, W), BF),
            pltpu.VMEM((NP + 1, 4, 3, 720, W), BF),
            pltpu.VMEM((5, 2, T, DB), BF),
            pltpu.VMEM((5, 2, DB, T), BF),
            pltpu.VMEM((DB, 4 * DB), BF),
            pltpu.VMEM((DB, 4 * DB), BF),
            pltpu.VMEM((4 * DB, DB), BF),
            pltpu.VMEM((4, DB, HALF), BF),
            pltpu.VMEM((4, DB, HALF), BF),
            pltpu.VMEM((4, HALF, DB), BF),
            pltpu.VMEM((5, T, DB), F32),
            pltpu.VMEM((5, 4, TB, DB), BF),
            pltpu.VMEM((5, 4, TB, DB), BF),
            pltpu.VMEM((5, 4, TB, DB), BF),
            pltpu.VMEM((5, 4, TB, DB), BF),
            pltpu.VMEM((4, TB, DB), BF),
            pltpu.VMEM((4, TB, DB), BF),
            dma((3, 4, 2)), dma((4,)), dma((4,)), dma((3, 4)), dma((3, 4)),
            dma((5, 4)), dma((5, 4)), dma((5, 4)), dma((5, 4)),
            dma((NP + 1, 8, 4)), dma((NP + 1, 8, 4)), dma((3, NP, 4)), dma((3, NP, 4)),
            dma((3, NP + 1, 4)), dma((5, 5)), dma((5, 5)),
            pltpu.SemaphoreType.REGULAR((NP + 1, 4, 4)),
        ],
        compiler_params=pltpu.CompilerParams(
            collective_id=0, has_side_effects=True, vmem_limit_bytes=63 * 2**20
        ),
        cost_estimate=pl.CostEstimate(
            flops=16 * T * DB * FB, bytes_accessed=12 * DB * FB, transcendentals=T * FB
        ),
    )(layer_input, out_grad, head_depth.reshape(1, TB), gate_weight, up_weight, down_weight)
    return pl.pallas_call(
        copy_kernel,
        out_shape=[jax.ShapeDtypeStruct(out.shape, out.dtype) for out in outs],
        in_specs=[hbm] * 4,
        out_specs=[hbm] * 4,
        scratch_shapes=[pltpu.VMEM(out.shape, out.dtype) for out in outs] + [dma((2, 13))],
        compiler_params=pltpu.CompilerParams(vmem_limit_bytes=63 * 2**20),
        cost_estimate=pl.CostEstimate(flops=0, bytes_accessed=12 * DB * FB, transcendentals=0),
    )(*outs)


def solution(mesh):
    in_specs = (
        P("col", "row"),
        P("col", "row"),
        P("col"),
        P("row", "col"),
        P("row", "col"),
        P("col", "row"),
    )
    out_specs = (P("col", "row"), P("row", "col"), P("row", "col"), P("col", "row"))
    return jax.shard_map(body, mesh=mesh, in_specs=in_specs, out_specs=out_specs, check_vma=False)
```

```python
import jax
import jax.numpy as jnp
from jax import lax
from jax.experimental import pallas as pl
from jax.experimental.pallas import tpu as pltpu
from jax.sharding import PartitionSpec as P

MESH = pl.DeviceIdType.MESH
BF = jnp.bfloat16
F32 = jnp.float32

T = 768
DB = 512
FB = 3584
TB = 96
PART = FB // 4
HALF = 384
W = 128
NP = 3
ROFF = ((0, 384, 576, 672), (0, 0, 384, 576))

ORDER = (
    ("relay", 0), ("relay", 1), ("all", 3), ("turn", 0), ("relay", 2), ("near", 0, 0), ("near", 0, 1), ("turn", 1), ("relay", 3),
    ("near", 1, 0), ("near", 1, 1), ("turn", 2), ("relay", 4), ("near", 2, 0), ("near", 2, 1),
    ("near", 0, 2), ("near", 1, 2), ("near", 2, 2), ("near", 3, 0), ("near", 3, 1), ("near", 3, 2), ("send", 1),
    ("keep", 0), ("keep", 1), ("keep", 2), ("keep", 3),
    ("rs", 3, 0), ("rs", 0, 1), ("send", 2), ("rs", 3, 1), ("rs", 0, 2),
    ("rs", 1, 1), ("rs", 3, 2), ("rs", 0, 3), ("rs", 1, 2), ("rs", 3, 3), ("rs", 2, 1),
    ("ag", 0, 3), ("rs", 1, 3), ("rs", 2, 2), ("ag", 0, 2), ("ag", 1, 3), ("turn", 3), ("rs", 2, 3),
    ("ag", 1, 2), ("ag", 3, 3), ("turn", 4), ("ag", 2, 3),
    ("ag", 0, 1), ("in", 0), ("ag", 2, 2), ("theirs", 0), ("ag", 3, 2), ("ag", 1, 1), ("in", 1),
    ("ag", 2, 1), ("ag", 3, 1), ("in", 2), ("fold", 1), ("fold", 2), ("fold", 3), ("fold", 4), ("theirs", 1),
    ("theirs", 2), ("own", 0), ("ag", 3, 0), ("in", 3), ("own", 1), ("fold", 0), ("own", 2), ("own", 3),
)


def nt(a, b):
    return lax.dot_general(a, b, (((1,), (1,)), ((), ())), preferred_element_type=F32)


def nn(a, b):
    return jnp.dot(a, b, preferred_element_type=F32)


def kernel(
    x_ref, og_ref, hd_ref, wg_hbm, wu_hbm, wd_hbm,
    gi_ref, dg_hbm, du_hbm, dd_hbm,
    S, R, XS, XT, WG, WU, WD, QG, QU, QD, GI, GB, CR, HS, ZR, YS, YR,
    wsem, xs, xr, qs, qr, zs, zr, cs, cr, ss, sr, gs, gr, osem, hs, hr, free,
):
    row = lax.axis_index("row")
    col = lax.axis_index("col")
    x = lax.rem(row, 4)
    y = row // 4
    z = col // 2
    c = lax.rem(col, 2)
    rows_of = (
        y * 4 + x + 1 - 2 * lax.rem(x, 2),
        (y + 1 - 2 * lax.rem(y, 2)) * 4 + x,
        y * 4 + 3 - x,
        (3 - y) * 4 + x,
    )
    bits = (lax.rem((x + 1) // 2, 2), lax.rem((y + 1) // 2, 2), x // 2, y // 2)

    def pick(values, d):
        return jnp.where(d == 0, values[0], jnp.where(d == 1, values[1], jnp.where(d == 2, values[2], values[3])))

    def near(d):
        return (pick(rows_of, lax.rem(d, 4)), col)

    def along_z(dz):
        return (row, lax.rem(z + dz, 4) * 2 + c)

    other_core = (row, z * 2 + 1 - c)

    def first(j):
        return 0 if j == NP else 1

    def size(j, k):
        return T >> (k + 1 - first(j))

    def low(j, p, k):
        at = jnp.int32(0)
        for i in range(first(j), k):
            at = at + pick(bits, lax.rem(p + i, 4)) * size(j, i)
        return at

    def rows(at, n):
        return pl.ds(pl.multiple_of(at, 48), n)

    def held(j, p):
        return pl.ds(pl.multiple_of(p * DB + j * W, W), W)

    def place(j, p):
        if j == NP:
            at = p * PART + 2 * HALF
        else:
            at = p * PART + pick(bits, p) * HALF + j * W
        return pl.ds(pl.multiple_of(at, W), W)

    def remote(src, dst, send, recv, device):
        return pltpu.make_async_remote_copy(
            src_ref=src, dst_ref=dst, send_sem=send, recv_sem=recv, device_id=device, device_id_type=MESH
        )

    def rs_copy(j, k, p):
        n = size(j, k)
        at = low(j, p, k) + (1 - pick(bits, lax.rem(p + k, 4))) * n
        return remote(
            S.at[j, p, :, rows(at, n)], R.at[j, p, :, pl.ds(ROFF[first(j)][k], n)],
            ss.at[j, k, p], sr.at[j, k, p], near(p + k),
        )

    def ag_copy(j, k, p):
        where = S.at[j, p, :, rows(low(j, p, k + 1), size(j, k))]
        return remote(where, where, ss.at[j, 7 - k, p], sr.at[j, 7 - k, p], near(p + k))

    def load_copies(p):
        copies = []
        for i, (at, n, to) in enumerate(
            ((p * PART + pick(bits, p) * HALF, HALF, p * DB), (p * PART + 2 * HALF, W, p * DB + HALF))
        ):
            src = pl.ds(pl.multiple_of(at, W), n)
            dst = pl.ds(pl.multiple_of(to, W), n)
            copies.append(pltpu.make_async_copy(wg_hbm.at[:, src], WG.at[:, dst], wsem.at[0, p, i]))
            copies.append(pltpu.make_async_copy(wu_hbm.at[:, src], WU.at[:, dst], wsem.at[1, p, i]))
            copies.append(pltpu.make_async_copy(wd_hbm.at[src], WD.at[dst], wsem.at[2, p, i]))
        return copies

    def weight_copies(p):
        at = pl.ds(pl.multiple_of(p * PART + (1 - pick(bits, p)) * HALF, W), HALF)
        return (
            remote(wg_hbm.at[:, at], QG.at[p], qs.at[0, p], qr.at[0, p], near(p)),
            remote(wu_hbm.at[:, at], QU.at[p], qs.at[1, p], qr.at[1, p], near(p)),
            remote(wd_hbm.at[at], QD.at[p], qs.at[2, p], qr.at[2, p], near(p)),
        )

    mine = pl.ds(pl.multiple_of(col * TB, TB), TB)

    def x_copy(d):
        return remote(XS.at[0, :, mine], XS.at[1 + d, :, mine], xs.at[d], xr.at[d], near(d))

    def block(dz):
        return pl.ds(pl.multiple_of((lax.rem(z + dz + 4, 4) * 2 + c) * TB, TB), TB)

    def z_copy(b, dz):
        where = XS.at[b, :, mine]
        return remote(where, where, zs.at[b, dz], zr.at[b, dz], along_z(dz))

    def z_relay(b, dz):
        where = XS.at[b, dz // 2, block(-dz)]
        return remote(where, where, zs.at[b, dz - 1], zr.at[b, dz - 1], along_z(dz))

    def c_copy(b, dz):
        where = XS.at[b, :, block(-dz)]
        return remote(where, where, cs.at[b, dz], cr.at[b, dz], other_core)

    barrier = pltpu.get_barrier_semaphore()
    for device in [near(d) for d in range(4)] + [along_z(dz) for dz in (1, 2, 3)] + [other_core]:
        pl.semaphore_signal(barrier, inc=1, device_id=device, device_id_type=MESH)

    @pl.loop(0, 4)
    def _(p):
        for copy in load_copies(p):
            copy.start()

    depth = jnp.broadcast_to(hd_ref[...], (128, TB))
    weight = jnp.ones((128, TB), F32)
    for level in range(1, 5):
        weight = jnp.where(depth == level, F32(0.8) ** level, weight)
    weight = weight.T
    XS[0, 0, mine, :] = x_ref[...]
    for i in range(DB // 128):
        at = slice(i * 128, (i + 1) * 128)
        XS[0, 1, mine, at] = (og_ref[:, at].astype(F32) * weight).astype(BF)

    pl.semaphore_wait(barrier, 8)

    for d in range(4):
        x_copy(d).start()
    for dz in (1, 3):
        z_copy(0, dz).start()
    c_copy(0, 0).start()
    for p in range(4):
        for copy in weight_copies(p):
            copy.start()
    GI[...] = jnp.zeros_like(GI)

    def z_send(b):
        for dz in (1, 3):
            z_copy(b, dz).start()

    def relay(b):
        for dz in (1, 3):
            z_copy(b, dz).wait_recv()
            z_relay(b, dz).start()
            c_copy(b, dz).start()
        if b == 0:
            for d in range(4):
                x_copy(d).wait_recv()
                c_copy(1 + d, 0).start()
                if d < 2:
                    z_send(1 + d)
        elif b < 3:
            z_send(b + 2)

    def gathered(b):
        for dz in (1, 3):
            z_relay(b, dz).wait_recv()
        c_copy(b, 2).start()
        for dz in range(4):
            c_copy(b, dz).wait_recv()

    def joined(parts):
        return jnp.concatenate(parts, axis=1)

    def forward_near(p, m, at):
        r = rows(at, T // 2)
        cols = pl.ds(p * DB, HALF)
        if m < 2:
            near_w, own_w = ((QG, WG), (QU, WU))[m]
            part = nn(XS[0, 0, r, :], own_w[:, cols]) + nn(XS[1 + p, 0, r, :], near_w[p])
        else:
            part = nt(XS[0, 1, r, :], WD[cols, :]) + nt(XS[1 + p, 1, r, :], QD[p])
        for j in range(NP):
            S[j, p, m, r, :] = part[:, j * W : (j + 1) * W].astype(BF)

    def forward_all():
        gate_w = joined([WG[:, held(NP, p)] for p in range(4)])
        up_w = joined([WU[:, held(NP, p)] for p in range(4)])
        back_w = jnp.concatenate([WD[held(NP, p), :] for p in range(4)], axis=0)
        for i in range(2):
            r = slice(i * (T // 2), (i + 1) * (T // 2))
            parts = (nn(XS[0, 0, r, :], gate_w), nn(XS[0, 0, r, :], up_w), nt(XS[0, 1, r, :], back_w))
            for m, part in enumerate(parts):
                for p in range(4):
                    S[NP, p, m, r, :] = part[:, p * W : (p + 1) * W].astype(BF)

    def send(j):
        @pl.loop(0, 4)
        def _(p):
            rs_copy(j, first(j), p).start()

    def fwd_near(p, m):
        if m == 0:
            gathered(1 + p)
        weight_copies(p)[m].wait_recv()
        bit = pick(bits, lax.rem(p + 1, 4))
        forward_near(p, m, (1 - bit) * (T // 2))
        if m == 2:
            rs_copy(0, 1, p).start()
        else:
            forward_near(p, m, bit * (T // 2))

    def fwd_kept(p):
        forward_near(p, 2, pick(bits, lax.rem(p + 1, 4)) * (T // 2))

    def rs(j, k):
        n = size(j, k)
        step = min(n, 96)

        @pl.loop(0, 4)
        def _(p):
            rs_copy(j, k, p).wait_recv()
            at = low(j, p, k + 1)
            off = ROFF[first(j)][k]
            if k < 3:
                @pl.loop(0, n // step)
                def _(i):
                    r = rows(at + i * step, step)
                    q = rows(off + i * step, step)
                    S[j, p, :, r, :] = (S[j, p, :, r, :].astype(F32) + R[j, p, :, q, :].astype(F32)).astype(BF)

                rs_copy(j, k + 1, p).start()
            else:
                r = rows(at, n)
                q = pl.ds(off, n)
                gate = S[j, p, 0, r, :].astype(F32) + R[j, p, 0, q, :].astype(F32)
                up = S[j, p, 1, r, :].astype(F32) + R[j, p, 1, q, :].astype(F32)
                back = S[j, p, 2, r, :].astype(F32) + R[j, p, 2, q, :].astype(F32)
                sig = jax.nn.sigmoid(gate)
                silu = gate * sig
                S[j, p, 0, r, :] = (silu * up).astype(BF)
                S[j, p, 1, r, :] = (back * up * (sig * (1.0 + gate * (1.0 - sig)))).astype(BF)
                S[j, p, 2, r, :] = (back * silu).astype(BF)
            rs_copy(j, k, p).wait_send()
            pl.semaphore_signal(free.at[j, k, p], inc=1, device_id=near(p + k), device_id_type=MESH)

        if k == 3:
            @pl.loop(0, 4)
            def _(p):
                gather(j, 3, p)

    def gather(j, k, p):
        pl.semaphore_wait(free.at[j, k, p], 1)
        ag_copy(j, k, p).start()

    def ag(j, k):
        @pl.loop(0, 4)
        def _(p):
            ag_copy(j, k, p).wait_recv()
            if k > first(j):
                gather(j, k - 1, p)

    def own_copies(j, p):
        src, dst = held(j, p), place(j, p)
        return (
            pltpu.make_async_copy(WG.at[:, src], dg_hbm.at[:, dst], osem.at[0, j, p]),
            pltpu.make_async_copy(WU.at[:, src], du_hbm.at[:, dst], osem.at[1, j, p]),
            pltpu.make_async_copy(WD.at[src], dd_hbm.at[dst], osem.at[2, j, p]),
        )

    def near_copies(j, p):
        src, dst = pl.ds(j * W, W), place(j, p)
        return (
            remote(QG.at[p, :, src], dg_hbm.at[:, dst], gs.at[0, j, p], gr.at[0, j, p], near(p)),
            remote(QU.at[p, :, src], du_hbm.at[:, dst], gs.at[1, j, p], gr.at[1, j, p], near(p)),
            remote(QD.at[p, src], dd_hbm.at[dst], gs.at[2, j, p], gr.at[2, j, p], near(p)),
        )

    def input_grad(j):
        at = slice(j * W, (j + 1) * W)

        def acts(p, r):
            return [S[j, p, 1, r, :], S[j, p, 2, r, :]]

        if j < NP:
            @pl.loop(0, 4)
            def _(p):
                both = joined([QG[p, :, at], QU[p, :, at]])
                for i in range(3):
                    r = slice(i * 256, (i + 1) * 256)
                    GI[1 + p, r, :] = GI[1 + p, r, :] + nt(joined(acts(p, r)), both)
                if j == NP - 1:
                    gi_send(1 + p)

        weights = []
        for p in range(4):
            weights += [WG[:, held(j, p)], WU[:, held(j, p)]]
        weights = joined(weights)
        for i in range(3):
            r = slice(i * 256, (i + 1) * 256)
            GI[0, r, :] = GI[0, r, :] + nt(joined([a for p in range(4) for a in acts(p, r)]), weights)
        if j == NP:
            gi_send(0)

    def near_grads(j):
        at = slice(j * W, (j + 1) * W)

        @pl.loop(0, 4)
        def _(p):
            both = nn(XT[1 + p, 0], joined([S[j, p, 1], S[j, p, 2]])).astype(BF)
            QG[p, :, at] = both[:, :W]
            QU[p, :, at] = both[:, W:]
            QD[p, at, :] = nn(XT[1 + p, 1], S[j, p, 0]).astype(BF).T
            for copy in near_copies(j, p):
                copy.start()

    def own_grads(j):
        @pl.loop(0, 2)
        def _(i):
            for p in (2 * i, 2 * i + 1):
                both = nn(XT[0, 0], joined([S[j, p, 1], S[j, p, 2]])).astype(BF)
                WG[:, held(j, p)] = both[:, :W]
                WU[:, held(j, p)] = both[:, W:]
            down = nn(XT[0, 1], joined([S[j, 2 * i, 0], S[j, 2 * i + 1, 0]])).astype(BF)
            for n, p in enumerate((2 * i, 2 * i + 1)):
                WD[held(j, p), :] = down[:, n * W : (n + 1) * W].T
                for copy in own_copies(j, p):
                    copy.start()

    def tokens(zz, cc):
        return pl.ds(pl.multiple_of((zz * 2 + cc) * TB, TB), TB)

    def gi_core(b):
        return remote(GB.at[b], CR.at[b], hs.at[0, b], hr.at[0, b], other_core)

    def gi_z(b, dz):
        return remote(HS.at[b, dz], ZR.at[b, dz], hs.at[dz, b], hr.at[dz, b], along_z(dz))

    def gi_near(d):
        return remote(YS.at[d], YR.at[d], hs.at[4, d], hr.at[4, d], near(d))

    def gi_send(b):
        for zz in range(4):
            GB[b, zz] = GI[b, tokens(zz, 1 - c), :].astype(BF)
        gi_core(b).start()

    def gi_fold(b):
        gi_core(b).wait_recv()
        for dz in (1, 3, 2):
            zz = lax.rem(z + dz, 4)
            HS[b, dz] = (GI[b, tokens(zz, c), :] + CR[b, zz].astype(F32)).astype(BF)
            gi_z(b, dz).start()

    def gi_total(b):
        total = GI[b, mine, :] + CR[b, z].astype(F32)
        for dz in (1, 3, 2):
            gi_z(b, dz).wait_recv()
            total = total + ZR[b, dz].astype(F32)
        return total

    for what, j, *level in ORDER:
        if what == "relay":
            relay(j)
        elif what == "all":
            gathered(0)
            for p in range(4):
                for copy in load_copies(p):
                    copy.wait()
            forward_all()
            send(NP)
        elif what == "send":
            send(j)
        elif what == "near":
            fwd_near(j, level[0])
        elif what == "keep":
            fwd_kept(j)
        elif what == "turn":
            XT[j, 0] = XS[j, 0].T
            XT[j, 1] = XS[j, 1].T
        elif what == "rs":
            rs(j, level[0])
        elif what == "ag":
            ag(j, level[0])
        elif what == "in":
            input_grad(j)
        elif what == "fold":
            gi_fold(j)
        elif what == "theirs":
            near_grads(j)
        else:
            own_grads(j)

    @pl.loop(0, 4)
    def _(d):
        YS[d] = gi_total(1 + d).astype(BF)
        gi_near(d).start()

    total = gi_total(0)
    for d in range(4):
        gi_near(d).wait_recv()
        total = total + YR[d].astype(F32)
    gi_ref[...] = total.astype(BF)

    @pl.loop(0, 4)
    def _(p):
        x_copy(p).wait_send()
        gi_near(p).wait_send()
        for copy in weight_copies(p):
            copy.wait_send()
        for j in range(NP + 1):
            for copy in own_copies(j, p):
                copy.wait()
            for k in range(first(j), 4):
                ag_copy(j, k, p).wait_send()
            if j < NP:
                for copy in near_copies(j, p):
                    copy.wait()

    @pl.loop(0, 5)
    def _(b):
        gi_core(b).wait_send()
        for dz in range(4):
            c_copy(b, dz).wait_send()
            if dz > 0:
                gi_z(b, dz).wait_send()
        for dz in (1, 3):
            z_copy(b, dz).wait_send()
            z_relay(b, dz).wait_send()


def copy_kernel(a, b, c, d, out_a, out_b, out_c, out_d, held_a, held_b, held_c, held_d, sem):
    pieces = [(a, held_a, out_a)]
    for src, mid, dst in ((b, held_b, out_b), (c, held_c, out_c), (d, held_d, out_d)):
        n = src.shape[0] // 4
        for k in range(4):
            at = pl.ds(k * n, n)
            pieces.append((src.at[at], mid.at[at], dst.at[at]))
    reads = [pltpu.make_async_copy(src, mid, sem.at[0, i]) for i, (src, mid, dst) in enumerate(pieces)]
    writes = [pltpu.make_async_copy(mid, dst, sem.at[1, i]) for i, (src, mid, dst) in enumerate(pieces)]
    for read in reads:
        read.start()
    for read, write in zip(reads, writes):
        read.wait()
        write.start()
    for write in writes:
        write.wait()


def body(layer_input, out_grad, head_depth, gate_weight, up_weight, down_weight):
    vmem = pl.BlockSpec(memory_space=pltpu.VMEM)
    hbm = pl.BlockSpec(memory_space=pl.ANY)
    dma = pltpu.SemaphoreType.DMA
    outs = pl.pallas_call(
        kernel,
        out_shape=(
            jax.ShapeDtypeStruct((TB, DB), BF),
            jax.ShapeDtypeStruct((DB, FB), BF),
            jax.ShapeDtypeStruct((DB, FB), BF),
            jax.ShapeDtypeStruct((FB, DB), BF),
        ),
        in_specs=[vmem, vmem, vmem, hbm, hbm, hbm],
        out_specs=(vmem, hbm, hbm, hbm),
        scratch_shapes=[
            pltpu.VMEM((NP + 1, 4, 3, T, W), BF),
            pltpu.VMEM((NP + 1, 4, 3, 720, W), BF),
            pltpu.VMEM((5, 2, T, DB), BF),
            pltpu.VMEM((5, 2, DB, T), BF),
            pltpu.VMEM((DB, 4 * DB), BF),
            pltpu.VMEM((DB, 4 * DB), BF),
            pltpu.VMEM((4 * DB, DB), BF),
            pltpu.VMEM((4, DB, HALF), BF),
            pltpu.VMEM((4, DB, HALF), BF),
            pltpu.VMEM((4, HALF, DB), BF),
            pltpu.VMEM((5, T, DB), F32),
            pltpu.VMEM((5, 4, TB, DB), BF),
            pltpu.VMEM((5, 4, TB, DB), BF),
            pltpu.VMEM((5, 4, TB, DB), BF),
            pltpu.VMEM((5, 4, TB, DB), BF),
            pltpu.VMEM((4, TB, DB), BF),
            pltpu.VMEM((4, TB, DB), BF),
            dma((3, 4, 2)), dma((4,)), dma((4,)), dma((3, 4)), dma((3, 4)),
            dma((5, 4)), dma((5, 4)), dma((5, 4)), dma((5, 4)),
            dma((NP + 1, 8, 4)), dma((NP + 1, 8, 4)), dma((3, NP, 4)), dma((3, NP, 4)),
            dma((3, NP + 1, 4)), dma((5, 5)), dma((5, 5)),
            pltpu.SemaphoreType.REGULAR((NP + 1, 4, 4)),
        ],
        compiler_params=pltpu.CompilerParams(
            collective_id=0, has_side_effects=True, vmem_limit_bytes=63 * 2**20
        ),
        cost_estimate=pl.CostEstimate(
            flops=16 * T * DB * FB, bytes_accessed=12 * DB * FB, transcendentals=T * FB
        ),
    )(layer_input, out_grad, head_depth.reshape(1, TB), gate_weight, up_weight, down_weight)
    return pl.pallas_call(
        copy_kernel,
        out_shape=[jax.ShapeDtypeStruct(out.shape, out.dtype) for out in outs],
        in_specs=[hbm] * 4,
        out_specs=[hbm] * 4,
        scratch_shapes=[pltpu.VMEM(out.shape, out.dtype) for out in outs] + [dma((2, 13))],
        compiler_params=pltpu.CompilerParams(vmem_limit_bytes=63 * 2**20),
        cost_estimate=pl.CostEstimate(flops=0, bytes_accessed=12 * DB * FB, transcendentals=0),
    )(*outs)


def solution(mesh):
    in_specs = (
        P("col", "row"),
        P("col", "row"),
        P("col"),
        P("row", "col"),
        P("row", "col"),
        P("col", "row"),
    )
    out_specs = (P("col", "row"), P("row", "col"), P("row", "col"), P("col", "row"))
    return jax.shard_map(body, mesh=mesh, in_specs=in_specs, out_specs=out_specs, check_vma=False)
```
